128 devices in a mesh: grid: 64 (over x, y, z_lo, core), col: 2 (over z_hi).
Axes of the slice: x: 4, y: 4, z: 4 (z_hi: 2, z_lo: 2; z = z_hi * 2 + z_lo), core: 2. Of those that a mesh axis runs over, the one named last changes fastest.
Arguments:
- orbitals: bfloat16 [884736, 256], P(('grid', 'col')), may hold values from -6 to 6
- points: int32 [1024], replicated, may hold values from 0 to 884735, as said below
- cinv: bfloat16 [1024, 256], replicated, may hold values from -0.1875 to 0.1875
Outputs:
- potential: bfloat16 [256, 884736], P(None, ('grid', 'col'))
- coupling: float32 [1024, 256], P(('grid', 'col'))
The draws below stay inside these ranges and needn't reach their ends.
Inputs may be any that keep to these rules, and one draw needn't show every extreme that they name: `points`: 1024 distinct grid rows.
All inputs are finite; a program needn't handle non-finite values.
Results may differ from the reference program's by a relative error of at most 0.0046.
Values may be sent and summed in bfloat16 or wider, within the bound.
A program may use at most 192 MiB of HBM per device.

```python
import math
import jax
import jax.numpy as jnp
from jax import lax

NX = 96
NORB = 256
NMU = 1024
NCOL = 256
NGRID = 884736


def draw_points(key, part):
    order = jax.random.permutation(jax.random.fold_in(key, 7), NX ** 3)
    return order[:NMU].astype(jnp.int32)


def block_levels(stream_key, extent, split, least, high):
    factor_of, own = 1.0, jax.random.fold_in(stream_key, 6)
    for dim, shards_of in split:
        draws = jnp.exp(jax.random.uniform(jax.random.fold_in(own, dim), (shards_of,), jnp.float32, least / len(split), high / len(split)))
        factor_of = factor_of * jnp.repeat(draws, extent[dim] // shards_of).reshape([-1 if axis == dim else 1 for axis in range(len(extent))])
    return factor_of


def gaussian(stream_key, shape, width, reach, pieces=(), held_as=jnp.bfloat16):
    array = jax.random.normal(stream_key, shape, jnp.float32) * width
    if len(pieces) > 0:
        array = block_levels(stream_key, shape, pieces, -0.22, 0.18) * array
    return jnp.clip(array, min=-reach, max=reach).astype(held_as)


def setup_inputs(seed: int = 0) -> dict:
    seeds = jax.random.split(jax.random.key(seed), 4)
    return {
        "orbitals": gaussian(seeds[0], (NGRID, NORB), 1.0, 6.0, ((0, 128),)),
        "points": draw_points(jax.random.fold_in(seeds[3], 71), 0),
        "cinv": gaussian(seeds[2], (NMU, NCOL), NMU ** -0.5, 0.1875),
    }


screening = 0.25

def kernel_table(dtype):
    index = jnp.arange(NX)
    wave = jnp.where(index < (NX + 1) // 2, index, index - NX).astype(dtype) * (2.0 * math.pi / NX)
    squared = wave[:, None, None] ** 2 + wave[None, :, None] ** 2 + wave[None, None, :] ** 2
    return jnp.where(squared > 0, 1.0 / (squared + screening), 0.0).astype(dtype)

def reference(orbitals, points, cinv):
    point_rows = orbitals[points]
    scale = 1.0 / math.sqrt(NORB)

    def pair_of(block):
        product = jnp.dot(block, point_rows.T, preferred_element_type=jnp.float32) * scale
        return (product * product).astype(jnp.bfloat16)
    blocks = orbitals.reshape(NX, NX * NX, NORB)

    def fit(block):
        return jnp.dot(pair_of(block), cinv, preferred_element_type=jnp.float32)
    theta = lax.map(fit, blocks)
    fields = jnp.moveaxis(theta.reshape(NX, NX, NX, NCOL), 3, 0)
    table = kernel_table(theta.dtype)

    def solve(field):
        return jnp.fft.ifftn(table * jnp.fft.fftn(field)).real.astype(jnp.bfloat16)
    potential = lax.map(solve, fields).reshape(NCOL, NX ** 3)
    pot_blocks = jnp.moveaxis(potential.reshape(NCOL, NX, NX * NX), 1, 0)

    def accumulate(total, inputs):
        block, pots = inputs
        return (total + jnp.dot(pair_of(block).T, pots.T, preferred_element_type=jnp.float32), None)
    total, _ = lax.scan(accumulate, jnp.zeros((NMU, NCOL), jnp.float32), (blocks, pot_blocks))
    coupling = total * (math.sqrt(NMU) / NX ** 3)
    return (potential, coupling)
```

```python
import functools
import math

import jax
import jax.numpy as jnp
from jax import lax
from jax.experimental import pallas as pl
from jax.experimental.pallas import tpu as pltpu
from jax.sharding import PartitionSpec as P

NX = 96
RANKS = 128
AXES = ("grid", "col")
MESH = pl.DeviceIdType.MESH

screening = 0.25


def rank_id():
    return lax.axis_index("grid") * 2 + lax.axis_index("col")


def device(rank):
    return {"grid": rank // 2, "col": rank % 2}


def exchange_kernel(spread, x_ref, o_ref, send_sem, recv_sem, own_sem):
    me = rank_id()

    def to(k):
        return (me + k * 37) % RANKS

    def source(rank):
        return x_ref if spread else x_ref.at[rank]

    barrier = pltpu.get_barrier_semaphore()

    def greet(k, _):
        pl.semaphore_signal(barrier, inc=1, device_id=device(to(k)), device_id_type=MESH)
        return 0

    lax.fori_loop(1, RANKS, greet, 0)
    own = pltpu.make_async_copy(source(me), o_ref.at[me], own_sem)
    own.start()
    pl.semaphore_wait(barrier, RANKS - 1)

    def send(k, _):
        rank = to(k)
        pltpu.make_async_remote_copy(
            src_ref=source(rank),
            dst_ref=o_ref.at[me],
            send_sem=send_sem.at[k],
            recv_sem=recv_sem.at[k],
            device_id=device(rank),
            device_id_type=MESH,
        ).start()
        return 0

    lax.fori_loop(1, RANKS, send, 0)

    def settle(k, _):
        rank = (me + (RANKS - k) * 37) % RANKS
        copy = pltpu.make_async_remote_copy(
            src_ref=source(rank),
            dst_ref=o_ref.at[rank],
            send_sem=send_sem.at[k],
            recv_sem=recv_sem.at[k],
            device_id=device(rank),
            device_id_type=MESH,
        )
        copy.wait()
        return 0

    lax.fori_loop(1, RANKS, settle, 0)
    own.wait()


def exchange(x, collective_id, spread=False):
    shape = (RANKS, *x.shape) if spread else x.shape
    return pl.pallas_call(
        functools.partial(exchange_kernel, spread),
        out_shape=jax.ShapeDtypeStruct(shape, x.dtype),
        in_specs=[pl.BlockSpec(memory_space=pltpu.VMEM)],
        out_specs=pl.BlockSpec(memory_space=pltpu.VMEM),
        scratch_shapes=[
            pltpu.SemaphoreType.DMA((RANKS,)),
            pltpu.SemaphoreType.DMA((RANKS,)),
            pltpu.SemaphoreType.DMA,
        ],
        compiler_params=pltpu.CompilerParams(
            collective_id=collective_id, has_side_effects=True, vmem_limit_bytes=16 * 2**20
        ),
    )(x)


def scatter_sum(x, collective_id):
    rows = x.shape[0] // RANKS
    blocks = exchange(x.reshape(RANKS, rows * 2, 128), collective_id)
    return jnp.sum(blocks.astype(jnp.float32), axis=0).reshape(rows, 256)


def kernel_table(size):
    index = jnp.arange(size)
    wave = jnp.where(index < (size + 1) // 2, index, index - size).astype(jnp.float32) * (
        2.0 * math.pi / size
    )
    squared = wave[:, None, None] ** 2 + wave[None, :, None] ** 2 + wave[None, None, :] ** 2
    return jnp.where(squared > 0, 1.0 / (squared + screening), 0.0)


def along(table, values, axis):
    forms = {1: "kn,cnyz->ckyz", 2: "kn,cxnz->cxkz", 3: "kn,cxyn->cxyk"}
    return jnp.einsum(forms[axis], table, values, precision=lax.Precision.HIGHEST)


def screened_solve(field):
    size = field.shape[1]
    index = jnp.arange(size, dtype=jnp.int32)
    phase = index[:, None] * index[None, :] % size
    angle = phase.astype(jnp.float32) * (2.0 * math.pi / size)
    table = (jnp.cos(angle) + jnp.sin(angle)) / math.sqrt(size)
    for axis in (3, 2, 1):
        field = along(table, field, axis)
    field = field * kernel_table(size)
    for axis in (1, 2, 3):
        field = along(table, field, axis)
    return field


def local(orbitals, points, cinv):
    local_rows, orbital_count = orbitals.shape
    npoints, columns = cinv.shape
    per_rank = columns // RANKS
    first_row = rank_id() * local_rows
    offset = points - first_row
    inside = (offset >= 0) & (offset < local_rows)
    picked = jnp.take(orbitals, jnp.clip(offset, 0, local_rows - 1), axis=0)
    picked = jnp.where(inside[:, None], picked, jnp.zeros_like(picked))
    mine = scatter_sum(picked, 0).astype(jnp.bfloat16)
    point_rows = exchange(mine.reshape(16, 128), 1, spread=True).reshape(npoints, orbital_count)
    scale = 1.0 / math.sqrt(orbital_count)
    product = (
        lax.dot_general(
            orbitals, point_rows, (((1,), (1,)), ((), ())), preferred_element_type=jnp.float32
        )
        * scale
    )
    pairs = (product * product).astype(jnp.bfloat16)
    theta_cols = lax.dot_general(
        cinv, pairs, (((0,), (1,)), ((), ())), preferred_element_type=jnp.float32
    ).astype(jnp.bfloat16)
    fields = lax.all_to_all(theta_cols, AXES, split_axis=0, concat_axis=1, tiled=True)
    fields = fields.reshape(per_rank, NX, NX, NX).astype(jnp.float32)
    potentials = screened_solve(fields).astype(jnp.bfloat16).reshape(per_rank, NX**3)
    rows_back = lax.all_to_all(potentials, AXES, split_axis=1, concat_axis=0, tiled=True)
    factor = math.sqrt(npoints) / float(NX**3)
    partial = (
        lax.dot_general(
            pairs, rows_back, (((0,), (1,)), ((), ())), preferred_element_type=jnp.float32
        )
        * factor
    )
    coupling = scatter_sum(partial.astype(jnp.bfloat16), 2)
    return (rows_back, coupling)


def solution(mesh):
    in_specs = (P(AXES, None), P(), P())
    out_specs = (P(None, AXES), P(AXES, None))
    return jax.shard_map(local, mesh=mesh, in_specs=in_specs, out_specs=out_specs, check_vma=False)
```

```python
import functools
import math

import jax
import jax.numpy as jnp
import ml_dtypes
import numpy as np
from jax import lax
from jax.experimental import pallas as pl
from jax.experimental.pallas import tpu as pltpu
from jax.sharding import PartitionSpec as P

NX = 96
NMU = 1024
RANKS = 128
CHIPS = 64
LINES = 8
TILE = LINES * NX
OWN = 72
PAD = 80
AXES = ("grid", "col")
MESH = pl.DeviceIdType.MESH

screening = 0.25


def rank_id():
    return lax.axis_index("grid") * 2 + lax.axis_index("col")


def device(rank):
    return {"grid": rank // 2, "col": lax.rem(rank, 2)}


def basis(size):
    index = np.arange(size)
    angle = (index[:, None] * index[None, :] % size) * (2.0 * math.pi / size)
    return (np.cos(angle) + np.sin(angle)) / math.sqrt(size)


def two_terms(table):
    high = table.astype(np.float32).astype(ml_dtypes.bfloat16)
    low = (table - high.astype(np.float64)).astype(np.float32).astype(ml_dtypes.bfloat16)
    return high, low


def line_tables():
    table = np.einsum("pc,lm->plmc", basis(NX), np.eye(LINES)).reshape(TILE, TILE)
    return two_terms(table)


def split(values):
    high = values.astype(jnp.bfloat16)
    return high, (values - high.astype(jnp.float32)).astype(jnp.bfloat16)


def dot(a, b):
    return jnp.dot(a, b, preferred_element_type=jnp.float32)


def twice(high):
    return jnp.concatenate([high, high], axis=0)


def parity_of(pair):
    return lax.rem(pair // 8 + pair // 2 + pair, 2)


def owner(p, half):
    pair = p - CHIPS
    first = p // 2 * 4 + lax.rem(p, 2)
    second = pair * 4 + 2 + lax.rem(half + parity_of(jnp.maximum(pair, 0)), 2)
    return jnp.where(p < CHIPS, first, second)


def whole_kernel(
    picked_ref, cinv_ref, basis_ref, terms_ref, orb_hbm, high_hbm, low_hbm,
    pot_ref, part_ref,
    orb, high, low, pair, hat0, hat1, send0, send1, recv0, recv1, field, back0, back1,
    rows, gathered, mine, spread, parts, middle, total, turned,
    sum_sem, all_sem, forth_sem, back_sem, own_sem, load_sem,
):
    hats, sends, recvs, backs = (hat0, hat1), (send0, send1), (recv0, recv1), (back0, back1)
    me = rank_id()
    chip = me // 4 * 2 + lax.rem(me, 2)
    core = lax.rem(me // 2, 2)
    my_p = jnp.where(core == 0, chip, CHIPS + chip // 2)
    my_half = lax.rem(parity_of(chip // 2) + lax.rem(chip, 2), 2)

    loads = [
        pltpu.make_async_copy(source, target, load_sem.at[i])
        for i, (source, target) in enumerate(((orb_hbm, orb), (high_hbm, high), (low_hbm, low)))
    ]
    for load in loads:
        load.start()

    def peer(k):
        return lax.rem(me + k * 37, RANKS)

    barrier = pltpu.get_barrier_semaphore()

    def greet(k, _):
        pl.semaphore_signal(barrier, inc=1, device_id=device(peer(k)), device_id_type=MESH)
        return 0

    lax.fori_loop(1, RANKS, greet, 0)
    pl.semaphore_wait(barrier, RANKS - 1)

    def remote(source, target, sems, rank):
        return pltpu.make_async_remote_copy(
            src_ref=source,
            dst_ref=target,
            send_sem=sems.at[0],
            recv_sem=sems.at[1],
            device_id=device(rank),
            device_id_type=MESH,
        )

    def bytes_of(ref, count, sem):
        block = ref.at[pl.ds(0, count)]
        pltpu.make_async_copy(block, block, sem).wait()

    def exchange(source_of, target, sems, local_sem):
        local = pltpu.make_async_copy(source_of(me), target.at[me], local_sem)
        local.start()

        def go(k, _):
            rank = peer(k)
            remote(source_of(rank), target.at[me], sems, rank).start()
            return 0

        lax.fori_loop(1, RANKS, go, 0)
        local.wait()
        bytes_of(target, RANKS - 1, sems.at[0])
        bytes_of(target, RANKS - 1, sems.at[1])

    exchange(lambda d: picked_ref.at[d], gathered, sum_sem.at[0], own_sem.at[0])
    mine[...] = jnp.sum(gathered[...].astype(jnp.float32), axis=0).astype(jnp.bfloat16)
    exchange(lambda d: mine, spread, all_sem, own_sem.at[1])

    def place(i, _):
        parts_of = [spread[2 * i + j].astype(jnp.float32) for j in range(2)]
        block = [jnp.concatenate([b[:8], b[8:]], axis=1) for b in parts_of]
        rows[pl.ds(pl.multiple_of(16 * i, 16), 16), :] = jnp.concatenate(block, axis=0).astype(jnp.bfloat16)
        return 0

    lax.fori_loop(0, RANKS // 2, place, 0)
    norms = jnp.sum(jnp.square(rows[...].astype(jnp.float32)), axis=1, keepdims=True)
    weights = norms * (jnp.sum(norms) * (1.0 / (NMU * 65536.0)))
    mean = jnp.sum(weights * cinv_ref[...].astype(jnp.float32), axis=0, keepdims=True)

    for load in loads:
        load.wait()

    def fit(step, _):
        here = pl.ds(pl.multiple_of(step * TILE, TILE), TILE)
        product = lax.dot_general(
            orb[here, :], rows[...], (((1,), (1,)), ((), ())), preferred_element_type=jnp.float32
        ) * (1.0 / 16.0)
        squared = (product * product).astype(jnp.bfloat16)
        pair[here, :] = squared
        theta = dot(squared, cinv_ref[...]) - mean
        top, rest = split(theta)
        block = dot(high[...], top) + (dot(low[...], top) + dot(high[...], rest))
        block = block.reshape(NX, LINES, 256)
        lines = pl.ds(pl.multiple_of(step * LINES, LINES), LINES)
        hat0[:, lines, :] = block[:, :, :128]
        hat1[:, lines, :] = block[:, :, 128:]
        return 0

    lax.fori_loop(0, OWN // LINES, fit, 0)

    first_p = me * NX // RANKS

    for half in range(2):
        active = (core == 0) | (my_half == half)
        hat, sent, landed, sems = hats[half], sends[half], recvs[half], forth_sem.at[half]

        def pack(p, _, hat=hat, sent=sent):
            block = jnp.concatenate([hat[p], jnp.zeros((PAD - OWN, 128), jnp.float32)], axis=0)
            sent[p] = block.astype(jnp.bfloat16)
            return 0

        lax.fori_loop(0, NX, pack, 0)

        def go(k, _, sent=sent, landed=landed, sems=sems, half=half):
            p = lax.rem(first_p + k * 37, NX)
            rank = owner(p, half)

            @pl.when(rank != me)
            def _():
                remote(sent.at[p], landed.at[me], sems, rank).start()

            return 0

        lax.fori_loop(0, NX, go, 0)

        @pl.when(active)
        def _(sent=sent, landed=landed, half=half):
            pltpu.make_async_copy(sent.at[my_p], landed.at[me], own_sem.at[2 + half]).start()

    unit = 2.0 * math.pi / NX

    def signed(index):
        return jnp.where(index < NX // 2, index, index - NX).astype(jnp.float32) * unit

    along_a = signed(lax.broadcasted_iota(jnp.int32, (NX, NX), 1))
    along_c = signed(jnp.full((NX, NX), my_p, jnp.int32))
    base = along_a * along_a + along_c * along_c

    def build(kb, _):
        along_b = signed(jnp.full((NX, NX), kb, jnp.int32))
        squared = base + along_b * along_b
        weight = jnp.where(squared > 0, 1.0 / (squared + screening), 0.0)
        top, rest = split(basis_ref[...] * weight)
        table = terms_ref[...]
        full = dot(top, table[:, :NX]) + (dot(top, table[:, NX:]) + dot(rest, table[:, :NX]))
        top, rest = split(full)
        middle[kb] = jnp.concatenate([top, rest], axis=1)
        return 0

    lax.fori_loop(0, NX // 2 + 1, build, 0)

    for half in range(2):
        active = (core == 0) | (my_half == half)
        sent, landed, sems = sends[half], recvs[half], forth_sem.at[half]

        @pl.when(active)
        def _(sent=sent, landed=landed, sems=sems, half=half):
            bytes_of(landed, RANKS - 1, sems.at[1])
            bytes_of(sent, NX - 1, sems.at[0])
            pltpu.make_async_copy(sent.at[my_p], landed.at[me], own_sem.at[2 + half]).wait()
            solve(landed, field, middle, terms_ref)
            pltpu.make_async_copy(landed.at[me], backs[half].at[my_p], own_sem.at[4 + half]).start()

            def go(k, _):
                rank = peer(k)
                remote(landed.at[rank], backs[half].at[my_p], back_sem.at[half], rank).start()
                return 0

            lax.fori_loop(1, RANKS, go, 0)

        @pl.when(jnp.logical_not(active))
        def _(sent=sent, sems=sems):
            bytes_of(sent, NX, sems.at[0])

    for half in range(2):
        active = (core == 0) | (my_half == half)
        back, hat = backs[half], hat0

        @pl.when(active)
        def _(back=back, half=half):
            bytes_of(back, NX - 1, back_sem.at[half, 1])
            pltpu.make_async_copy(recvs[half].at[me], back.at[my_p], own_sem.at[4 + half]).wait()

        @pl.when(jnp.logical_not(active))
        def _(back=back, half=half):
            bytes_of(back, NX, back_sem.at[half, 1])

        def unpack(p, _, back=back, hat=hat):
            hat[p] = back[p].astype(jnp.float32)[:OWN]
            return 0

        lax.fori_loop(0, NX, unpack, 0)

        def finish(i, _, hat=hat, half=half):
            turns = []
            for t in range(3):
                lines = pl.ds(pl.multiple_of((3 * i + t) * LINES, LINES), LINES)
                turns.append(hat[:, lines, :].reshape(TILE, 128).T)
            block = jnp.concatenate(turns, axis=0).astype(jnp.bfloat16)
            pot = (dot(block, high[...]) + dot(block, low[...])).astype(jnp.bfloat16)
            term = None
            for t in range(3):
                here = pl.ds(pl.multiple_of((3 * i + t) * TILE, TILE), TILE)
                part = pot[128 * t : 128 * t + 128]
                pot_ref[pl.ds(128 * half, 128), here] = part
                product = dot(part, pair[here, :])
                term = product if term is None else term + product
            total[...] = jnp.where(i == 0, 0.0, total[...]) + term
            return 0

        lax.fori_loop(0, OWN // LINES // 3, finish, 0)
        turned[half] = total[...].T * (math.sqrt(NMU) / float(NX**3))

        @pl.when(active)
        def _(half=half):
            bytes_of(recvs[half], RANKS - 1, back_sem.at[half, 0])

    def lay(d, _):
        here = pl.ds(pl.multiple_of(8 * d, 8), 8)
        parts[d] = jnp.concatenate([turned[0, here, :], turned[1, here, :]], axis=0).astype(jnp.bfloat16)
        return 0

    lax.fori_loop(0, RANKS, lay, 0)
    exchange(lambda d: parts.at[d], spread, sum_sem.at[1], own_sem.at[6])
    part_ref[...] = jnp.sum(spread[...].astype(jnp.float32), axis=0)


def solve(landed, field, middle, terms_ref):
    def rows_of(u, plane):
        return pl.ds(pl.multiple_of(288 * u + 96 * plane, 96), 96)

    def forward(i, _):
        wholes = [
            jnp.concatenate([landed[8 * i + 4 * j + v].astype(jnp.float32)[:OWN] for v in range(4)], axis=0)
            for j in range(2)
        ]
        for plane in range(3):
            values = jnp.concatenate([w[96 * plane : 96 * plane + 96] for w in wholes], axis=1)
            result = dot(terms_ref[...], twice(values.astype(jnp.bfloat16)))
            for j in range(2):
                field[rows_of(2 * i + j, plane), :] = result[:, 128 * j : 128 * j + 128]
        return 0

    lax.fori_loop(0, 16, forward, 0)

    def across(kb, other):
        table = middle[kb]
        places = [pl.ds(at, NX, stride=NX) for at in (kb, other)]
        top, rest = split(jnp.concatenate([field[place, :] for place in places], axis=1))
        result = dot(table, twice(top)) + dot(table[:, :NX], rest)
        for j in range(2):
            field[places[j], :] = result[:, 128 * j : 128 * j + 128]

    def alone(kb):
        table, place = middle[kb], pl.ds(kb, NX, stride=NX)
        top, rest = split(field[place, :])
        field[place, :] = dot(table, twice(top)) + dot(table[:, :NX], rest)

    def inner(i, _):
        for j in range(2):
            kb = 2 * i + 1 + j
            across(kb, NX - kb)
        return 0

    lax.fori_loop(0, 23, inner, 0)
    across(47, 49)
    alone(0)
    alone(48)

    def backward(i, _):
        planes = []
        for plane in range(3):
            values = jnp.concatenate([field[rows_of(2 * i + j, plane), :] for j in range(2)], axis=1)
            top, rest = split(values)
            planes.append(dot(terms_ref[...], twice(top)) + dot(terms_ref[:, :NX], rest))
        whole = jnp.concatenate(planes, axis=0)
        for j in range(2):
            for v in range(4):
                part = whole[OWN * v : OWN * v + OWN, 128 * j : 128 * j + 128]
                part = jnp.concatenate([part, jnp.zeros((PAD - OWN, 128), jnp.float32)], axis=0)
                landed[8 * i + 4 * j + v] = part.astype(jnp.bfloat16)
        return 0

    lax.fori_loop(0, 16, backward, 0)


def everything(picked, cinv, orbitals):
    table = basis(NX)
    high, low = line_tables()
    terms = np.concatenate(two_terms(table), axis=1)
    vmem = pl.BlockSpec(memory_space=pltpu.VMEM)
    hbm = pl.BlockSpec(memory_space=pl.ANY)
    bf, f32 = jnp.bfloat16, jnp.float32
    local_rows = orbitals.shape[0]
    dma = pltpu.SemaphoreType.DMA
    return pl.pallas_call(
        whole_kernel,
        out_shape=(
            jax.ShapeDtypeStruct((256, local_rows), bf),
            jax.ShapeDtypeStruct((16, 128), f32),
        ),
        in_specs=[vmem] * 4 + [hbm] * 3,
        out_specs=(vmem, vmem),
        scratch_shapes=[
            pltpu.VMEM((local_rows, 256), bf),
            pltpu.VMEM((TILE, TILE), bf),
            pltpu.VMEM((TILE, TILE), bf),
            pltpu.VMEM((local_rows, NMU), bf),
            pltpu.VMEM((NX, OWN, 128), f32),
            pltpu.VMEM((NX, OWN, 128), f32),
            pltpu.VMEM((NX, PAD, 128), bf),
            pltpu.VMEM((NX, PAD, 128), bf),
            pltpu.VMEM((RANKS, PAD, 128), bf),
            pltpu.VMEM((RANKS, PAD, 128), bf),
            pltpu.VMEM((NX * NX, 128), f32),
            pltpu.VMEM((NX, PAD, 128), bf),
            pltpu.VMEM((NX, PAD, 128), bf),
            pltpu.VMEM((NMU, 256), bf),
            pltpu.VMEM((RANKS, 16, 128), bf),
            pltpu.VMEM((16, 128), bf),
            pltpu.VMEM((RANKS, 16, 128), bf),
            pltpu.VMEM((RANKS, 16, 128), bf),
            pltpu.VMEM((NX // 2 + 1, NX, 2 * NX), bf),
            pltpu.VMEM((128, NMU), f32),
            pltpu.VMEM((2, NMU, 128), f32),
            dma((2, 2)),
            dma((2,)),
            dma((2, 2)),
            dma((2, 2)),
            dma((7,)),
            dma((3,)),
        ],
        compiler_params=pltpu.CompilerParams(
            collective_id=0, has_side_effects=True, vmem_limit_bytes=58 * 2**20
        ),
    )(
        picked, cinv, jnp.asarray(table.astype(np.float32)), jnp.asarray(terms),
        orbitals, jnp.asarray(high), jnp.asarray(low),
    )


def local(orbitals, points, cinv):
    local_rows, orbital_count = orbitals.shape
    offset = points - rank_id() * local_rows
    inside = (offset >= 0) & (offset < local_rows)
    picked = jnp.take(orbitals, jnp.clip(offset, 0, local_rows - 1), axis=0)
    picked = jnp.where(inside[:, None], picked, jnp.zeros_like(picked))
    picked = picked.reshape(RANKS, 8, 2, 128).swapaxes(1, 2).reshape(RANKS, 16, 128)
    potential, part = everything(picked, cinv, orbitals)
    return (potential, jnp.concatenate([part[:8], part[8:]], axis=1))


def solution(mesh):
    in_specs = (P(AXES, None), P(), P())
    out_specs = (P(None, AXES), P(AXES, None))
    return jax.shard_map(local, mesh=mesh, in_specs=in_specs, out_specs=out_specs, check_vma=False)
```

```python
import functools
import math

import jax
import jax.numpy as jnp
import ml_dtypes
import numpy as np
from jax import lax
from jax.experimental import pallas as pl
from jax.experimental.pallas import tpu as pltpu
from jax.sharding import PartitionSpec as P

NX = 96
NMU = 1024
RANKS = 128
CHIPS = 64
LINES = 8
TILE = LINES * NX
OWN = 72
MAIN = 64
BLOCK = 144
AXES = ("grid", "col")
MESH = pl.DeviceIdType.MESH

screening = 0.25


def rank_id():
    return lax.axis_index("grid") * 2 + lax.axis_index("col")


def device(rank):
    return {"grid": rank // 2, "col": lax.rem(rank, 2)}


def basis(size):
    index = np.arange(size)
    angle = (index[:, None] * index[None, :] % size) * (2.0 * math.pi / size)
    return (np.cos(angle) + np.sin(angle)) / math.sqrt(size)


def two_terms(table):
    high = table.astype(np.float32).astype(ml_dtypes.bfloat16)
    low = (table - high.astype(np.float64)).astype(np.float32).astype(ml_dtypes.bfloat16)
    return high, low


def line_tables():
    table = np.einsum("pc,lm->plmc", basis(NX), np.eye(LINES)).reshape(TILE, TILE)
    return two_terms(table)


def split(values):
    high = values.astype(jnp.bfloat16)
    return high, (values - high.astype(jnp.float32)).astype(jnp.bfloat16)


def dot(a, b):
    return jnp.dot(a, b, preferred_element_type=jnp.float32)


def twice(high):
    return jnp.concatenate([high, high], axis=0)


def parity_of(pair):
    return lax.rem(pair // 8 + pair // 2 + pair, 2)


def owner(p, half):
    pair = p - CHIPS
    first = p // 2 * 4 + lax.rem(p, 2)
    second = pair * 4 + 2 + lax.rem(half + parity_of(jnp.maximum(pair, 0)), 2)
    return jnp.where(p < CHIPS, first, second)


def whole_kernel(
    offset_ref, cinv_ref, basis_ref, terms_ref, orb_hbm, high_hbm, low_hbm,
    pot_ref, part_ref,
    orb, high, low, pair, sent, landed, field, back, back_tail,
    rows, picked, gathered, mine, spread, parts, middle, total, wide,
    sum_sem, all_sem, forth_sem, back_sem, own_sem, load_sem,
):
    me = rank_id()
    chip = me // 4 * 2 + lax.rem(me, 2)
    core = lax.rem(me // 2, 2)
    my_p = jnp.where(core == 0, chip, CHIPS + chip // 2)
    my_half = lax.rem(parity_of(chip // 2) + lax.rem(chip, 2), 2)
    on_first, on_second = core == 0, core == 1

    loads = [
        pltpu.make_async_copy(source, target, load_sem.at[i])
        for i, (source, target) in enumerate(((orb_hbm, orb), (high_hbm, high), (low_hbm, low)))
    ]
    for load in loads:
        load.start()

    def peer(k):
        return lax.rem(me + k * 37, RANKS)

    barrier = pltpu.get_barrier_semaphore()

    def greet(k, _):
        pl.semaphore_signal(barrier, inc=1, device_id=device(peer(k)), device_id_type=MESH)
        return 0

    lax.fori_loop(1, RANKS, greet, 0)

    def remote(source, target, send_sem, recv_sem, rank):
        return pltpu.make_async_remote_copy(
            src_ref=source,
            dst_ref=target,
            send_sem=send_sem,
            recv_sem=recv_sem,
            device_id=device(rank),
            device_id_type=MESH,
        )

    def bytes_of(ref, count, size, sem):
        block = ref.at[pl.ds(0, count), pl.ds(0, size), :]
        pltpu.make_async_copy(block, block, sem).wait()

    def exchange(source_of, target, sems, local_sem):
        local = pltpu.make_async_copy(source_of(me), target.at[me], local_sem)
        local.start()

        def go(k, _):
            rank = peer(k)
            remote(source_of(rank), target.at[me], sems.at[0], sems.at[1], rank).start()
            return 0

        lax.fori_loop(1, RANKS, go, 0)
        local.wait()
        bytes_of(target, RANKS - 1, 16, sems.at[0])
        bytes_of(target, RANKS - 1, 16, sems.at[1])

    def to_blocks(values):
        halves = [values[:, 128 * h : 128 * h + 128].reshape(RANKS, 8, 128) for h in range(2)]
        return jnp.concatenate(halves, axis=1)

    loads[0].wait()
    wide[...] = jnp.zeros_like(wide)

    def pick(step, _):
        here = pl.ds(pl.multiple_of(step * TILE, TILE), TILE)
        block = orb[here, :]
        for part in range(4):
            some = pl.ds(256 * part, 256)
            index = lax.broadcasted_iota(jnp.int32, (256, TILE), 1)
            match = index == (offset_ref[some, :] - step * TILE)
            wide[some, :] += dot(jnp.where(match, 1.0, 0.0).astype(jnp.bfloat16), block)
        return 0

    lax.fori_loop(0, OWN // LINES, pick, 0)
    picked[...] = to_blocks(wide[...]).astype(jnp.bfloat16)
    pl.semaphore_wait(barrier, RANKS - 1)
    exchange(lambda d: picked.at[d], gathered, sum_sem.at[0], own_sem.at[0])
    mine[...] = jnp.sum(gathered[...].astype(jnp.float32), axis=0).astype(jnp.bfloat16)
    exchange(lambda d: mine, spread, all_sem, own_sem.at[1])
    whole = spread[...].astype(jnp.float32)
    whole = [whole[:, 8 * h : 8 * h + 8].reshape(NMU, 128) for h in range(2)]
    rows[...] = jnp.concatenate(whole, axis=1).astype(jnp.bfloat16)
    norms = jnp.sum(jnp.square(rows[...].astype(jnp.float32)), axis=1, keepdims=True)
    weights = norms * (jnp.sum(norms) * (1.0 / (NMU * 65536.0)))
    mean = jnp.sum(weights * cinv_ref[...].astype(jnp.float32), axis=0, keepdims=True)

    def eight(step):
        here = pl.ds(pl.multiple_of(step * TILE, TILE), TILE)
        product = lax.dot_general(
            orb[here, :], rows[...], (((1,), (1,)), ((), ())), preferred_element_type=jnp.float32
        ) * (1.0 / 16.0)
        squared = (product * product).astype(jnp.bfloat16)
        pair[here, :] = squared
        theta = dot(squared, cinv_ref[...]) - mean
        results = []
        for line in range(LINES):
            top, rest = split(theta[NX * line : NX * line + NX])
            results.append(dot(terms_ref[...], twice(top)) + dot(terms_ref[:, :NX], rest))
        return [
            jnp.swapaxes(jnp.stack([r[:, 128 * h : 128 * h + 128] for r in results], axis=0), 0, 1)
            for h in range(2)
        ]

    def fit(step, _):
        first, second = eight(2 * step), eight(2 * step + 1)
        for h, base in enumerate((0, MAIN + 16)):
            lines = pl.ds(pl.multiple_of(base + 16 * step, 16), 16)
            sent[:, lines, :] = jnp.concatenate([first[h], second[h]], axis=1).astype(jnp.bfloat16)
        return 0

    first_p = me * NX // RANKS

    def forth(half, part):
        def go(k, _):
            p = lax.rem(first_p + k * 37, NX)
            rank = owner(p, half)

            def start(begin, size, sem):
                lines = pl.ds(begin, size)
                sems = forth_sem.at[sem]
                remote(sent.at[p, lines, :], landed.at[me, lines, :], sems.at[0], sems.at[1], rank).start()

            @pl.when(rank != me)
            def _():
                if part == 0:
                    start(0 if half == 0 else 80, 32, half)
                elif half == 0:
                    start(32, 48, 0)
                else:
                    start(112, 32, 1)

                    @pl.when(p >= CHIPS)
                    def _():
                        start(64, 16, 2)

            return 0

        lax.fori_loop(0, NX, go, 0)

    lax.fori_loop(0, 2, fit, 0)
    forth(0, 0)
    forth(1, 0)
    lax.fori_loop(2, 4, fit, 0)
    tail = eight(8)
    sent[:, pl.ds(MAIN, 16), :] = jnp.concatenate(tail, axis=1).astype(jnp.bfloat16)
    forth(0, 1)
    forth(1, 1)
    own_forth = pltpu.make_async_copy(sent.at[my_p], landed.at[me], own_sem.at[2])
    own_forth.start()

    unit = 2.0 * math.pi / NX

    def signed(index):
        return jnp.where(index < NX // 2, index, index - NX).astype(jnp.float32) * unit

    along_a = signed(lax.broadcasted_iota(jnp.int32, (NX, NX), 1))
    along_c = signed(jnp.full((NX, NX), my_p, jnp.int32))
    base = along_a * along_a + along_c * along_c

    def build(kb, _):
        along_b = signed(jnp.full((NX, NX), kb, jnp.int32))
        squared = base + along_b * along_b
        weight = jnp.where(squared > 0, 1.0 / (squared + screening), 0.0)
        top, rest = split(basis_ref[...] * weight)
        table = terms_ref[...]
        full = dot(top, table[:, :NX]) + (dot(top, table[:, NX:]) + dot(rest, table[:, :NX]))
        top, rest = split(full)
        middle[kb] = jnp.concatenate([top, rest], axis=1)
        return 0

    lax.fori_loop(0, NX // 2 + 1, build, 0)
    total[...] = jnp.zeros_like(total)
    loads[1].wait()
    loads[2].wait()
    own_forth.wait()

    def respond(half, rank):
        def start(begin, size, target, sem):
            source = landed.at[rank, pl.ds(begin, size), :]
            sems = back_sem.at[sem]
            remote(source, target, sems.at[0], sems.at[1], rank).start()

        def at(begin, size):
            return back.at[my_p, pl.ds(begin, size), :]

        @pl.when((rank != me) & on_first)
        def _():
            if half == 0:
                start(0, 64, at(0, 64), 0)
            else:
                start(64, 80, at(64, 80), 2)

        @pl.when((rank != me) & on_second)
        def _():
            if half == 0:
                start(0, 80, at(0, 80), 1)
            else:
                start(80, 64, at(80, 64), 3)
                start(64, 16, back_tail.at[chip // 2], 4)

    for half in range(2):
        active = on_first | (my_half == half)

        @pl.when(on_first)
        def _(half=half):
            bytes_of(landed, RANKS - 1, 80 if half == 0 else 64, forth_sem.at[half, 1])

        @pl.when(on_second & (my_half == half))
        def _(half=half):
            bytes_of(landed, RANKS - 1, 80 if half == 0 else 64, forth_sem.at[half, 1])
            if half == 1:
                bytes_of(landed, RANKS - 1, 16, forth_sem.at[2, 1])

        @pl.when(active)
        def _(half=half):
            solve(half, landed, field, middle, terms_ref, functools.partial(respond, half), me // 8)

    def keep(test, pieces):
        @pl.when(test)
        def _():
            for i, (begin, size, target) in enumerate(pieces):
                source = landed.at[me, pl.ds(begin, size), :]
                copy = pltpu.make_async_copy(source, target, own_sem.at[3 + i])
                copy.start()
                copy.wait()

    mine_back = lambda begin, size: (begin, size, back.at[my_p, pl.ds(begin, size), :])
    keep(on_first, [mine_back(0, BLOCK)])
    keep(on_second & (my_half == 0), [mine_back(0, 80)])
    keep(on_second & (my_half == 1), [mine_back(80, 64), (64, 16, back_tail.at[chip // 2])])

    def left(test, count, size, sem):
        @pl.when(test)
        def _():
            bytes_of(sent, count, size, forth_sem.at[sem, 0])

    owns = [on_first | (my_half == half) for half in range(2)]
    for half, size in ((0, 80), (1, 64)):
        left(owns[half], NX - 1, size, half)
        left(jnp.logical_not(owns[half]), NX, size, half)
    last = on_second & (my_half == 1)
    left(last, 31, 16, 2)
    left(jnp.logical_not(last), 32, 16, 2)

    def arrived(test, count, size, sem, ref):
        @pl.when(test)
        def _():
            bytes_of(ref, count, size, back_sem.at[sem, 1])

    def potentials(blocks, half, first):
        turns = [block.reshape(TILE, 128).T for block in blocks]
        block = jnp.concatenate(turns, axis=0).astype(jnp.bfloat16)
        pot = (dot(block, high[...]) + dot(block, low[...])).astype(jnp.bfloat16)
        term = None
        for t in range(len(blocks)):
            here = pl.ds(pl.multiple_of((first + t) * TILE, TILE), TILE)
            some = pot[128 * t : 128 * t + 128]
            pot_ref[pl.ds(128 * half, 128), here] = some
            product = dot(some, pair[here, :])
            term = product if term is None else term + product
        total[pl.ds(128 * half, 128), :] += term

    for half in range(2):
        second = on_second & (my_half == half)
        if half == 0:
            counts = ((0, 64, on_first, 64, back), (1, 32, second, 80, back))
        else:
            counts = ((2, 64, on_first, 80, back), (3, 32, second, 64, back), (4, 32, second, 16, back_tail))
        for sem, count, mine_too, size, ref in counts:
            arrived(mine_too, count - 1, size, sem, ref)
            arrived(jnp.logical_not(mine_too), count, size, sem, ref)

        def finish(s, _, half=half):
            lines = pl.ds(pl.multiple_of((80 if half else 0) + 16 * s, 16), 16)
            block = back[:, lines, :].astype(jnp.float32)
            potentials([block[:, :8], block[:, 8:]], half, 2 * s)
            return 0

        lax.fori_loop(0, 4, finish, 0)

    block = back[:, pl.ds(MAIN, 16), :].astype(jnp.float32)
    other = back_tail[...].astype(jnp.float32)
    potentials([block[:, :8]], 0, 8)
    potentials([jnp.concatenate([block[:CHIPS, 8:], other[:, 8:]], axis=0)], 1, 8)

    factor = math.sqrt(NMU) / float(NX**3)
    parts[...] = to_blocks(total[...].T * factor).astype(jnp.bfloat16)
    exchange(lambda d: parts.at[d], spread, sum_sem.at[1], own_sem.at[5])
    part_ref[...] = jnp.sum(spread[...].astype(jnp.float32), axis=0)

    def gone(test, size, sem):
        @pl.when(test)
        def _():
            bytes_of(landed, RANKS - 1, size, back_sem.at[sem, 0])

    gone(on_first, 64, 0)
    gone(on_first, 80, 2)
    gone(on_second & (my_half == 0), 80, 1)
    gone(on_second & (my_half == 1), 64, 3)
    gone(on_second & (my_half == 1), 16, 4)


def solve(half, landed, field, middle, terms_ref, respond, first):
    base = 80 if half else 0
    main, rest_of = pl.ds(base, MAIN), pl.ds(MAIN, 16)

    def block_of(rank):
        upper = landed[rank, main, :].astype(jnp.float32)
        lower = landed[rank, rest_of, :].astype(jnp.float32)[8 * half : 8 * half + 8]
        return jnp.concatenate([upper, lower], axis=0)

    def forward(i, _):
        for pack in range(2):
            start = 2 * i + pack
            wholes = [
                jnp.concatenate([block_of(8 * start + 4 * j + v) for v in range(4)], axis=0) for j in range(2)
            ]
            for plane in range(3):
                values = jnp.concatenate([w[96 * plane : 96 * plane + 96] for w in wholes], axis=1)
                result = dot(terms_ref[...], twice(values.astype(jnp.bfloat16)))
                for j in range(2):
                    field[3 * (2 * start + j) + plane] = result[:, 128 * j : 128 * j + 128]
        return 0

    lax.fori_loop(0, 8, forward, 0)

    def inner(i, _):
        place = pl.ds(pl.multiple_of(8 * i, 8), 8)
        values = jnp.swapaxes(field[:, place, :], 0, 1)
        results = []
        for j in range(8):
            kb = 8 * i + j
            table = middle[jnp.minimum(kb, NX - kb)]
            top, rest = split(values[j])
            results.append(dot(table, twice(top)) + dot(table[:, :NX], rest))
        field[:, place, :] = jnp.swapaxes(jnp.stack(results, axis=0), 0, 1)
        return 0

    lax.fori_loop(0, NX // 8, inner, 0)

    def backward(i, _):
        start = lax.rem(i + first, 16)
        planes = []
        for plane in range(3):
            values = jnp.concatenate([field[3 * (2 * start + j) + plane] for j in range(2)], axis=1)
            top, rest = split(values)
            planes.append(dot(terms_ref[...], twice(top)) + dot(terms_ref[:, :NX], rest))
        whole = jnp.concatenate(planes, axis=0)
        for j in range(2):
            for v in range(4):
                rank = 8 * start + 4 * j + v
                part = whole[OWN * v : OWN * v + OWN, 128 * j : 128 * j + 128]
                landed[rank, main, :] = part[:MAIN].astype(jnp.bfloat16)
                lower = landed[rank, rest_of, :].astype(jnp.float32)
                pieces = [part[MAIN:], lower[8:]] if half == 0 else [lower[:8], part[MAIN:]]
                landed[rank, rest_of, :] = jnp.concatenate(pieces, axis=0).astype(jnp.bfloat16)
        for v in range(8):
            respond(8 * start + v)
        return 0

    lax.fori_loop(0, 16, backward, 0)


def everything(offset, cinv, orbitals):
    table = basis(NX)
    high, low = line_tables()
    terms = np.concatenate(two_terms(table), axis=1)
    vmem = pl.BlockSpec(memory_space=pltpu.VMEM)
    hbm = pl.BlockSpec(memory_space=pl.ANY)
    bf, f32 = jnp.bfloat16, jnp.float32
    local_rows = orbitals.shape[0]
    dma = pltpu.SemaphoreType.DMA
    return pl.pallas_call(
        whole_kernel,
        out_shape=(
            jax.ShapeDtypeStruct((256, local_rows), bf),
            jax.ShapeDtypeStruct((16, 128), f32),
        ),
        in_specs=[vmem] * 4 + [hbm] * 3,
        out_specs=(vmem, vmem),
        scratch_shapes=[
            pltpu.VMEM((local_rows, 256), bf),
            pltpu.VMEM((TILE, TILE), bf),
            pltpu.VMEM((TILE, TILE), bf),
            pltpu.VMEM((local_rows, NMU), bf),
            pltpu.VMEM((NX, BLOCK, 128), bf),
            pltpu.VMEM((RANKS, BLOCK, 128), bf),
            pltpu.VMEM((NX, NX, 128), f32),
            pltpu.VMEM((NX, BLOCK, 128), bf),
            pltpu.VMEM((NX - CHIPS, 16, 128), bf),
            pltpu.VMEM((NMU, 256), bf),
            pltpu.VMEM((RANKS, 16, 128), bf),
            pltpu.VMEM((RANKS, 16, 128), bf),
            pltpu.VMEM((16, 128), bf),
            pltpu.VMEM((RANKS, 16, 128), bf),
            pltpu.VMEM((RANKS, 16, 128), bf),
            pltpu.VMEM((NX // 2 + 1, NX, 2 * NX), bf),
            pltpu.VMEM((256, NMU), f32),
            pltpu.VMEM((NMU, 256), f32),
            dma((2, 2)),
            dma((2,)),
            dma((3, 2)),
            dma((5, 2)),
            dma((6,)),
            dma((3,)),
        ],
        compiler_params=pltpu.CompilerParams(
            collective_id=0, has_side_effects=True, vmem_limit_bytes=58 * 2**20
        ),
    )(
        offset, cinv, jnp.asarray(table.astype(np.float32)), jnp.asarray(terms),
        orbitals, jnp.asarray(high), jnp.asarray(low),
    )


def local(orbitals, points, cinv):
    offset = points - rank_id() * orbitals.shape[0]
    potential, part = everything(offset.reshape(NMU, 1), cinv, orbitals)
    return (potential, jnp.concatenate([part[:8], part[8:]], axis=1))


def solution(mesh):
    in_specs = (P(AXES, None), P(), P())
    out_specs = (P(None, AXES), P(AXES, None))
    return jax.shard_map(local, mesh=mesh, in_specs=in_specs, out_specs=out_specs, check_vma=False)
```

```python
import functools
import math

import jax
import jax.numpy as jnp
import ml_dtypes
import numpy as np
from jax import lax
from jax.experimental import pallas as pl
from jax.experimental.pallas import tpu as pltpu
from jax.sharding import PartitionSpec as P

NX = 96
NMU = 1024
RANKS = 128
CHIPS = 64
LINES = 8
TILE = LINES * NX
OWN = 72
MAIN = 64
BLOCK = 144
AXES = ("grid", "col")
MESH = pl.DeviceIdType.MESH

screening = 0.25


def rank_id():
    return lax.axis_index("grid") * 2 + lax.axis_index("col")


def device(rank):
    return {"grid": rank // 2, "col": lax.rem(rank, 2)}


def basis(size):
    index = np.arange(size)
    angle = (index[:, None] * index[None, :] % size) * (2.0 * math.pi / size)
    return (np.cos(angle) + np.sin(angle)) / math.sqrt(size)


def two_terms(table):
    high = table.astype(np.float32).astype(ml_dtypes.bfloat16)
    low = (table - high.astype(np.float64)).astype(np.float32).astype(ml_dtypes.bfloat16)
    return high, low


def line_tables():
    table = np.einsum("pc,lm->plmc", basis(NX), np.eye(LINES)).reshape(TILE, TILE)
    return two_terms(table)


def split(values):
    high = values.astype(jnp.bfloat16)
    return high, (values - high.astype(jnp.float32)).astype(jnp.bfloat16)


def dot(a, b):
    return jnp.dot(a, b, preferred_element_type=jnp.float32)


def twice(high):
    return jnp.concatenate([high, high], axis=0)


def parity_of(pair):
    return lax.rem(pair // 8 + pair // 2 + pair, 2)


def owner(p, half):
    pair = p - CHIPS
    first = p // 2 * 4 + lax.rem(p, 2)
    second = pair * 4 + 2 + lax.rem(half + parity_of(jnp.maximum(pair, 0)), 2)
    return jnp.where(p < CHIPS, first, second)


def whole_kernel(
    points_ref, cinv_ref, basis_ref, terms_ref, orb_hbm, high_hbm, low_hbm,
    pot_hbm, part_ref,
    pot_ref, orb, high, low, pair, sent, landed, field, back, back_tail,
    rows, picked, gathered, mine, spread, parts, middle, total, wide,
    sum_sem, all_sem, forth_sem, back_sem, own_sem, load_sem,
):
    me = rank_id()
    chip = me // 4 * 2 + lax.rem(me, 2)
    core = lax.rem(me // 2, 2)
    my_p = jnp.where(core == 0, chip, CHIPS + chip // 2)
    my_half = lax.rem(parity_of(chip // 2) + lax.rem(chip, 2), 2)
    on_first, on_second = core == 0, core == 1

    loads = [
        pltpu.make_async_copy(source, target, load_sem.at[i])
        for i, (source, target) in enumerate(((orb_hbm, orb), (high_hbm, high), (low_hbm, low)))
    ]
    for load in loads:
        load.start()

    def peer(k):
        return lax.rem(me + k * 37, RANKS)

    barrier = pltpu.get_barrier_semaphore()

    def greet(k, _):
        pl.semaphore_signal(barrier, inc=1, device_id=device(peer(k)), device_id_type=MESH)
        return 0

    lax.fori_loop(1, RANKS, greet, 0)

    def remote(source, target, send_sem, recv_sem, rank):
        return pltpu.make_async_remote_copy(
            src_ref=source,
            dst_ref=target,
            send_sem=send_sem,
            recv_sem=recv_sem,
            device_id=device(rank),
            device_id_type=MESH,
        )

    def bytes_of(ref, count, size, sem):
        block = ref.at[pl.ds(0, count), pl.ds(0, size), :]
        pltpu.make_async_copy(block, block, sem).wait()

    def exchange(source_of, target, sems, local_sem):
        local = pltpu.make_async_copy(source_of(me), target.at[me], local_sem)
        local.start()

        def go(k, _):
            rank = peer(k)
            remote(source_of(rank), target.at[me], sems.at[0], sems.at[1], rank).start()
            return 0

        lax.fori_loop(1, RANKS, go, 0)
        local.wait()
        bytes_of(target, RANKS - 1, 16, sems.at[0])
        bytes_of(target, RANKS - 1, 16, sems.at[1])

    def to_blocks(values):
        halves = [values[:, 128 * h : 128 * h + 128].reshape(RANKS, 8, 128) for h in range(2)]
        return jnp.concatenate(halves, axis=1)

    loads[0].wait()
    wide[...] = jnp.zeros_like(wide)

    def pick(step, _):
        here = pl.ds(pl.multiple_of(step * TILE, TILE), TILE)
        block = orb[here, :]
        for part in range(4):
            some = pl.ds(256 * part, 256)
            index = lax.broadcasted_iota(jnp.int32, (256, TILE), 1)
            match = index == (points_ref[some, :] - (me * orb.shape[0] + step * TILE))
            wide[some, :] += dot(jnp.where(match, 1.0, 0.0).astype(jnp.bfloat16), block)
        return 0

    lax.fori_loop(0, OWN // LINES, pick, 0)
    picked[...] = to_blocks(wide[...]).astype(jnp.bfloat16)
    pl.semaphore_wait(barrier, RANKS - 1)
    exchange(lambda d: picked.at[d], gathered, sum_sem.at[0], own_sem.at[0])
    mine[...] = jnp.sum(gathered[...].astype(jnp.float32), axis=0).astype(jnp.bfloat16)
    exchange(lambda d: mine, spread, all_sem, own_sem.at[1])
    whole = spread[...].astype(jnp.float32)
    whole = [whole[:, 8 * h : 8 * h + 8].reshape(NMU, 128) for h in range(2)]
    rows[...] = jnp.concatenate(whole, axis=1).astype(jnp.bfloat16)
    norms = jnp.sum(jnp.square(rows[...].astype(jnp.float32)), axis=1, keepdims=True)
    weights = norms * (jnp.sum(norms) * (1.0 / (NMU * 65536.0)))
    mean = jnp.sum(weights * cinv_ref[...].astype(jnp.float32), axis=0, keepdims=True)

    def eight(step):
        here = pl.ds(pl.multiple_of(step * TILE, TILE), TILE)
        product = lax.dot_general(
            orb[here, :], rows[...], (((1,), (1,)), ((), ())), preferred_element_type=jnp.float32
        ) * (1.0 / 16.0)
        squared = (product * product).astype(jnp.bfloat16)
        pair[here, :] = squared
        theta = dot(squared, cinv_ref[...]) - mean
        results = []
        for line in range(LINES):
            top, rest = split(theta[NX * line : NX * line + NX])
            results.append(dot(terms_ref[...], twice(top)) + dot(terms_ref[:, :NX], rest))
        return [
            jnp.swapaxes(jnp.stack([r[:, 128 * h : 128 * h + 128] for r in results], axis=0), 0, 1)
            for h in range(2)
        ]

    def fit(step, _):
        first, second = eight(2 * step), eight(2 * step + 1)
        for h, base in enumerate((0, MAIN + 16)):
            lines = pl.ds(pl.multiple_of(base + 16 * step, 16), 16)
            sent[:, lines, :] = jnp.concatenate([first[h], second[h]], axis=1).astype(jnp.bfloat16)
        return 0

    first_p = me * NX // RANKS

    def forth(half, begin, size):
        def go(k, _):
            p = lax.rem(first_p + k * 37, NX)
            rank = owner(p, half)

            def start(begin, size, sem):
                lines = pl.ds(begin, size)
                sems = forth_sem.at[sem]
                remote(sent.at[p, lines, :], landed.at[me, lines, :], sems.at[0], sems.at[1], rank).start()

            if half == 0:
                pl.when(rank != me)(lambda: start(begin, size, 0))
            else:
                pl.when((rank != me) & (p < CHIPS))(lambda: start(80, 64, 1))
                pl.when((rank != me) & (p >= CHIPS))(lambda: start(64, 80, 2))
            return 0

        lax.fori_loop(0, NX, go, 0)

    def fit_and_send(step, _):
        fit(step, 0)
        pl.when(step == 0)(lambda: forth(0, 0, 16))
        pl.when(step == 2)(lambda: forth(0, 16, 32))
        return 0

    lax.fori_loop(0, 4, fit_and_send, 0)
    tail = eight(8)
    sent[:, pl.ds(MAIN, 16), :] = jnp.concatenate(tail, axis=1).astype(jnp.bfloat16)
    forth(0, 48, 32)
    forth(1, None, None)
    own_forth = pltpu.make_async_copy(sent.at[my_p], landed.at[me], own_sem.at[2])
    own_forth.start()

    unit = 2.0 * math.pi / NX

    def signed(index):
        return jnp.where(index < NX // 2, index, index - NX).astype(jnp.float32) * unit

    along_a = signed(lax.broadcasted_iota(jnp.int32, (NX, NX), 1))
    along_c = signed(jnp.full((NX, NX), my_p, jnp.int32))
    base = along_a * along_a + along_c * along_c

    def build(kb, _):
        along_b = signed(jnp.full((NX, NX), kb, jnp.int32))
        squared = base + along_b * along_b
        weight = jnp.where(squared > 0, 1.0 / (squared + screening), 0.0)
        top, rest = split(basis_ref[...] * weight)
        table = terms_ref[...]
        full = dot(top, table[:, :NX]) + (dot(top, table[:, NX:]) + dot(rest, table[:, :NX]))
        top, rest = split(full)
        middle[kb] = jnp.concatenate([top, rest], axis=1)
        return 0

    lax.fori_loop(0, NX // 2 + 1, build, 0)
    total[...] = jnp.zeros_like(total)
    loads[1].wait()
    loads[2].wait()
    own_forth.wait()

    def respond(half, rank):
        def start(begin, size, target, sem):
            source = landed.at[rank, pl.ds(begin, size), :]
            sems = back_sem.at[sem]
            remote(source, target, sems.at[0], sems.at[1], rank).start()

        def at(begin, size):
            return back.at[my_p, pl.ds(begin, size), :]

        @pl.when(on_first)
        def _():
            if half == 0:
                start(0, 64, at(0, 64), 0)
            else:
                start(64, 80, at(64, 80), 2)

        @pl.when(on_second)
        def _():
            if half == 0:
                start(0, 80, at(0, 80), 1)
            else:
                start(80, 64, at(80, 64), 3)
                start(64, 16, back_tail.at[chip // 2], 4)

    for half in range(2):
        active = on_first | (my_half == half)

        @pl.when(on_first)
        def _(half=half):
            bytes_of(landed, RANKS - 1, 80 if half == 0 else 64, forth_sem.at[half, 1])

        @pl.when(on_second & (my_half == half))
        def _(half=half):
            bytes_of(landed, RANKS - 1, 80, forth_sem.at[2 * half, 1])

        @pl.when(active)
        def _(half=half):
            solve(half, landed, field, middle, terms_ref)

            def answer(k, _):
                respond(half, peer(k))
                return 0

            lax.fori_loop(1, RANKS, answer, 0)

    def keep(test, pieces):
        @pl.when(test)
        def _():
            for i, (begin, size, target) in enumerate(pieces):
                source = landed.at[me, pl.ds(begin, size), :]
                copy = pltpu.make_async_copy(source, target, own_sem.at[3 + i])
                copy.start()
                copy.wait()

    mine_back = lambda begin, size: (begin, size, back.at[my_p, pl.ds(begin, size), :])
    keep(on_first, [mine_back(0, BLOCK)])
    keep(on_second & (my_half == 0), [mine_back(0, 80)])
    keep(on_second & (my_half == 1), [mine_back(80, 64), (64, 16, back_tail.at[chip // 2])])

    def left(test, count, size, sem):
        @pl.when(test)
        def _():
            bytes_of(sent, count, size, forth_sem.at[sem, 0])

    owns = on_first | (my_half == 0)
    left(owns, NX - 1, 80, 0)
    left(jnp.logical_not(owns), NX, 80, 0)
    left(on_first, CHIPS - 1, 64, 1)
    left(on_second, CHIPS, 64, 1)
    last = on_second & (my_half == 1)
    left(last, NX - CHIPS - 1, 80, 2)
    left(jnp.logical_not(last), NX - CHIPS, 80, 2)

    def arrived(test, count, size, sem, ref):
        @pl.when(test)
        def _():
            bytes_of(ref, count, size, back_sem.at[sem, 1])

    def potentials(blocks, half, first):
        turns = [block.reshape(TILE, 128).T for block in blocks]
        block = jnp.concatenate(turns, axis=0).astype(jnp.bfloat16)
        pot = (dot(block, high[...]) + dot(block, low[...])).astype(jnp.bfloat16)
        term = None
        for t in range(len(blocks)):
            here = pl.ds(pl.multiple_of((first + t) * TILE, TILE), TILE)
            some = pot[128 * t : 128 * t + 128]
            pot_ref[pl.ds(128 * half, 128), here] = some
            product = dot(some, pair[here, :])
            term = product if term is None else term + product
        total[pl.ds(128 * half, 128), :] += term

    for half in range(2):
        second = on_second & (my_half == half)
        if half == 0:
            counts = ((0, 64, on_first, 64, back), (1, 32, second, 80, back))
        else:
            counts = ((2, 64, on_first, 80, back), (3, 32, second, 64, back), (4, 32, second, 16, back_tail))
        for sem, count, mine_too, size, ref in counts:
            arrived(mine_too, count - 1, size, sem, ref)
            arrived(jnp.logical_not(mine_too), count, size, sem, ref)

        def finish(s, _, half=half):
            lines = pl.ds(pl.multiple_of((80 if half else 0) + 16 * s, 16), 16)
            block = back[:, lines, :].astype(jnp.float32)
            potentials([block[:, :8], block[:, 8:]], half, 2 * s)
            return 0

        lax.fori_loop(0, 4, finish, 0)

    block = back[:, pl.ds(MAIN, 16), :].astype(jnp.float32)
    other = back_tail[...].astype(jnp.float32)
    potentials([block[:, :8]], 0, 8)
    potentials([jnp.concatenate([block[:CHIPS, 8:], other[:, 8:]], axis=0)], 1, 8)

    store = pltpu.make_async_copy(pot_ref, pot_hbm, load_sem.at[3])
    store.start()

    factor = math.sqrt(NMU) / float(NX**3)
    parts[...] = to_blocks(total[...].T * factor).astype(jnp.bfloat16)
    exchange(lambda d: parts.at[d], spread, sum_sem.at[1], own_sem.at[5])
    share = jnp.sum(spread[...].astype(jnp.float32), axis=0)
    part_ref[...] = jnp.concatenate([share[:8], share[8:]], axis=1)
    store.wait()

    def gone(test, size, sem):
        @pl.when(test)
        def _():
            bytes_of(landed, RANKS - 1, size, back_sem.at[sem, 0])

    gone(on_first, 64, 0)
    gone(on_first, 80, 2)
    gone(on_second & (my_half == 0), 80, 1)
    gone(on_second & (my_half == 1), 64, 3)
    gone(on_second & (my_half == 1), 16, 4)


def solve(half, landed, field, middle, terms_ref):
    base = 80 if half else 0
    main, rest_of = pl.ds(base, MAIN), pl.ds(MAIN, 16)

    def block_of(rank):
        upper = landed[rank, main, :].astype(jnp.float32)
        lower = landed[rank, rest_of, :].astype(jnp.float32)[8 * half : 8 * half + 8]
        return jnp.concatenate([upper, lower], axis=0)

    def forward(i, _):
        for pack in range(2):
            start = 2 * i + pack
            wholes = [
                jnp.concatenate([block_of(8 * start + 4 * j + v) for v in range(4)], axis=0) for j in range(2)
            ]
            for plane in range(3):
                values = jnp.concatenate([w[96 * plane : 96 * plane + 96] for w in wholes], axis=1)
                result = dot(terms_ref[...], twice(values.astype(jnp.bfloat16)))
                for j in range(2):
                    field[3 * (2 * start + j) + plane] = result[:, 128 * j : 128 * j + 128]
        return 0

    lax.fori_loop(0, 8, forward, 0)

    def inner(i, _):
        place = pl.ds(pl.multiple_of(8 * i, 8), 8)
        values = jnp.swapaxes(field[:, place, :], 0, 1)
        results = []
        for j in range(8):
            kb = 8 * i + j
            table = middle[jnp.minimum(kb, NX - kb)]
            top, rest = split(values[j])
            results.append(dot(table, twice(top)) + dot(table[:, :NX], rest))
        field[:, place, :] = jnp.swapaxes(jnp.stack(results, axis=0), 0, 1)
        return 0

    lax.fori_loop(0, NX // 8, inner, 0)

    def backward(i, _):
        start = i
        planes = []
        for plane in range(3):
            values = jnp.concatenate([field[3 * (2 * start + j) + plane] for j in range(2)], axis=1)
            top, rest = split(values)
            planes.append(dot(terms_ref[...], twice(top)) + dot(terms_ref[:, :NX], rest))
        whole = jnp.concatenate(planes, axis=0)
        for j in range(2):
            for v in range(4):
                rank = 8 * start + 4 * j + v
                part = whole[OWN * v : OWN * v + OWN, 128 * j : 128 * j + 128]
                landed[rank, main, :] = part[:MAIN].astype(jnp.bfloat16)
                lower = landed[rank, rest_of, :].astype(jnp.float32)
                pieces = [part[MAIN:], lower[8:]] if half == 0 else [lower[:8], part[MAIN:]]
                landed[rank, rest_of, :] = jnp.concatenate(pieces, axis=0).astype(jnp.bfloat16)
        return 0

    lax.fori_loop(0, 16, backward, 0)


def everything(points, cinv, orbitals):
    table = basis(NX)
    high, low = line_tables()
    terms = np.concatenate(two_terms(table), axis=1)
    vmem = pl.BlockSpec(memory_space=pltpu.VMEM)
    hbm = pl.BlockSpec(memory_space=pl.ANY)
    bf, f32 = jnp.bfloat16, jnp.float32
    local_rows = orbitals.shape[0]
    dma = pltpu.SemaphoreType.DMA
    return pl.pallas_call(
        whole_kernel,
        out_shape=(
            jax.ShapeDtypeStruct((256, local_rows), bf),
            jax.ShapeDtypeStruct((8, 256), f32),
        ),
        in_specs=[vmem] * 4 + [hbm] * 3,
        out_specs=(hbm, vmem),
        scratch_shapes=[
            pltpu.VMEM((256, local_rows), bf),
            pltpu.VMEM((local_rows, 256), bf),
            pltpu.VMEM((TILE, TILE), bf),
            pltpu.VMEM((TILE, TILE), bf),
            pltpu.VMEM((local_rows, NMU), bf),
            pltpu.VMEM((NX, BLOCK, 128), bf),
            pltpu.VMEM((RANKS, BLOCK, 128), bf),
            pltpu.VMEM((NX, NX, 128), f32),
            pltpu.VMEM((NX, BLOCK, 128), bf),
            pltpu.VMEM((NX - CHIPS, 16, 128), bf),
            pltpu.VMEM((NMU, 256), bf),
            pltpu.VMEM((RANKS, 16, 128), bf),
            pltpu.VMEM((RANKS, 16, 128), bf),
            pltpu.VMEM((16, 128), bf),
            pltpu.VMEM((RANKS, 16, 128), bf),
            pltpu.VMEM((RANKS, 16, 128), bf),
            pltpu.VMEM((NX // 2 + 1, NX, 2 * NX), bf),
            pltpu.VMEM((256, NMU), f32),
            pltpu.VMEM((NMU, 256), f32),
            dma((2, 2)),
            dma((2,)),
            dma((3, 2)),
            dma((5, 2)),
            dma((6,)),
            dma((4,)),
        ],
        compiler_params=pltpu.CompilerParams(
            collective_id=0, has_side_effects=True, vmem_limit_bytes=58 * 2**20
        ),
    )(
        points, cinv, jnp.asarray(table.astype(np.float32)), jnp.asarray(terms),
        orbitals, jnp.asarray(high), jnp.asarray(low),
    )


def local(orbitals, points, cinv):
    return everything(points.reshape(NMU, 1), cinv, orbitals)


def solution(mesh):
    in_specs = (P(AXES, None), P(), P())
    out_specs = (P(None, AXES), P(AXES, None))
    return jax.shard_map(local, mesh=mesh, in_specs=in_specs, out_specs=out_specs, check_vma=False)
```

```python
import functools
import math

import jax
import jax.numpy as jnp
import ml_dtypes
import numpy as np
from jax import lax
from jax.experimental import pallas as pl
from jax.experimental.pallas import tpu as pltpu
from jax.sharding import PartitionSpec as P

NX = 96
NMU = 1024
RANKS = 128
CHIPS = 64
LINES = 8
TILE = LINES * NX
OWN = 72
MAIN = 64
BLOCK = 144
AXES = ("grid", "col")
MESH = pl.DeviceIdType.MESH

screening = 0.25


def rank_id():
    return lax.axis_index("grid") * 2 + lax.axis_index("col")


def device(rank):
    return {"grid": rank // 2, "col": lax.rem(rank, 2)}


def basis(size):
    index = np.arange(size)
    angle = (index[:, None] * index[None, :] % size) * (2.0 * math.pi / size)
    return (np.cos(angle) + np.sin(angle)) / math.sqrt(size)


def two_terms(table):
    high = table.astype(np.float32).astype(ml_dtypes.bfloat16)
    low = (table - high.astype(np.float64)).astype(np.float32).astype(ml_dtypes.bfloat16)
    return high, low


def line_tables():
    table = np.einsum("pc,lm->plmc", basis(NX), np.eye(LINES)).reshape(TILE, TILE)
    return two_terms(table)


def split(values):
    high = values.astype(jnp.bfloat16)
    return high, (values - high.astype(jnp.float32)).astype(jnp.bfloat16)


def dot(a, b):
    return jnp.dot(a, b, preferred_element_type=jnp.float32)


def twice(high):
    return jnp.concatenate([high, high], axis=0)


def parity_of(pair):
    return lax.rem(pair // 8 + pair // 2 + pair, 2)


def owner(p, half):
    pair = p - CHIPS
    first = p // 2 * 4 + lax.rem(p, 2)
    second = pair * 4 + 2 + lax.rem(half + parity_of(jnp.maximum(pair, 0)), 2)
    return jnp.where(p < CHIPS, first, second)


def whole_kernel(
    points_ref, cinv_ref, basis_ref, terms_ref, orb_hbm, high_hbm, low_hbm,
    pot_hbm, part_ref,
    pot_ref, orb, high, low, pair, sent, landed, field, back, back_tail,
    rows, picked, gathered, mine, spread, parts, middle, total, wide,
    sum_sem, all_sem, forth_sem, back_sem, own_sem, load_sem,
):
    me = rank_id()
    chip = me // 4 * 2 + lax.rem(me, 2)
    core = lax.rem(me // 2, 2)
    my_p = jnp.where(core == 0, chip, CHIPS + chip // 2)
    my_half = lax.rem(parity_of(chip // 2) + lax.rem(chip, 2), 2)
    on_first, on_second = core == 0, core == 1

    loads = [
        pltpu.make_async_copy(source, target, load_sem.at[i])
        for i, (source, target) in enumerate(((orb_hbm, orb), (high_hbm, high), (low_hbm, low)))
    ]
    for load in loads:
        load.start()

    def peer(k):
        return lax.rem(me + k * 53, RANKS)

    barrier = pltpu.get_barrier_semaphore()

    def greet(k, _):
        pl.semaphore_signal(barrier, inc=1, device_id=device(peer(k)), device_id_type=MESH)
        return 0

    lax.fori_loop(1, RANKS, greet, 0)

    def remote(source, target, send_sem, recv_sem, rank):
        return pltpu.make_async_remote_copy(
            src_ref=source,
            dst_ref=target,
            send_sem=send_sem,
            recv_sem=recv_sem,
            device_id=device(rank),
            device_id_type=MESH,
        )

    def bytes_of(ref, count, size, sem):
        block = ref.at[pl.ds(0, count), pl.ds(0, size), :]
        pltpu.make_async_copy(block, block, sem).wait()

    def exchange(source_of, target, sems, local_sem):
        local = pltpu.make_async_copy(source_of(me), target.at[me], local_sem)
        local.start()

        def go(k, _):
            rank = peer(k)
            remote(source_of(rank), target.at[me], sems.at[0], sems.at[1], rank).start()
            return 0

        lax.fori_loop(1, RANKS, go, 0)
        local.wait()
        bytes_of(target, RANKS - 1, 16, sems.at[0])
        bytes_of(target, RANKS - 1, 16, sems.at[1])

    def to_blocks(values):
        halves = [values[:, 128 * h : 128 * h + 128].reshape(RANKS, 8, 128) for h in range(2)]
        return jnp.concatenate(halves, axis=1)

    loads[0].wait()
    wide[...] = jnp.zeros_like(wide)

    def pick(step, _):
        here = pl.ds(pl.multiple_of(step * TILE, TILE), TILE)
        block = orb[here, :]
        for part in range(4):
            some = pl.ds(256 * part, 256)
            index = lax.broadcasted_iota(jnp.int32, (256, TILE), 1)
            match = index == (points_ref[some, :] - (me * orb.shape[0] + step * TILE))
            wide[some, :] += dot(jnp.where(match, 1.0, 0.0).astype(jnp.bfloat16), block)
        return 0

    lax.fori_loop(0, OWN // LINES, pick, 0)
    picked[...] = to_blocks(wide[...]).astype(jnp.bfloat16)
    pl.semaphore_wait(barrier, RANKS - 1)
    exchange(lambda d: picked.at[d], gathered, sum_sem.at[0], own_sem.at[0])
    mine[...] = jnp.sum(gathered[...].astype(jnp.float32), axis=0).astype(jnp.bfloat16)
    exchange(lambda d: mine, spread, all_sem, own_sem.at[1])
    whole = spread[...].astype(jnp.float32)
    whole = [whole[:, 8 * h : 8 * h + 8].reshape(NMU, 128) for h in range(2)]
    rows[...] = jnp.concatenate(whole, axis=1).astype(jnp.bfloat16)
    norms = jnp.sum(jnp.square(rows[...].astype(jnp.float32)), axis=1, keepdims=True)
    weights = norms * (jnp.sum(norms) * (1.0 / (NMU * 65536.0)))
    mean = jnp.sum(weights * cinv_ref[...].astype(jnp.float32), axis=0, keepdims=True)

    def eight(step):
        here = pl.ds(pl.multiple_of(step * TILE, TILE), TILE)
        product = lax.dot_general(
            orb[here, :], rows[...], (((1,), (1,)), ((), ())), preferred_element_type=jnp.float32
        ) * (1.0 / 16.0)
        squared = (product * product).astype(jnp.bfloat16)
        pair[here, :] = squared
        theta = dot(squared, cinv_ref[...]) - mean
        results = []
        for line in range(LINES):
            top, rest = split(theta[NX * line : NX * line + NX])
            results.append(dot(terms_ref[...], twice(top)) + dot(terms_ref[:, :NX], rest))
        return [
            jnp.swapaxes(jnp.stack([r[:, 128 * h : 128 * h + 128] for r in results], axis=0), 0, 1)
            for h in range(2)
        ]

    def fit(step, _):
        first, second = eight(2 * step), eight(2 * step + 1)
        for h, base in enumerate((0, MAIN + 16)):
            lines = pl.ds(pl.multiple_of(base + 16 * step, 16), 16)
            sent[:, lines, :] = jnp.concatenate([first[h], second[h]], axis=1).astype(jnp.bfloat16)
        return 0

    first_p = me * NX // RANKS

    def forth(half, begin, size):
        def go(k, _):
            p = lax.rem(first_p + k * 53, NX)
            rank = owner(p, half)

            def start(begin, size, sem):
                lines = pl.ds(begin, size)
                sems = forth_sem.at[sem]
                remote(sent.at[p, lines, :], landed.at[me, lines, :], sems.at[0], sems.at[1], rank).start()

            if half == 0:
                pl.when(rank != me)(lambda: start(begin, size, 0))
            else:
                pl.when((rank != me) & (p < CHIPS))(lambda: start(80, 64, 1))
                pl.when((rank != me) & (p >= CHIPS))(lambda: start(64, 80, 2))
            return 0

        lax.fori_loop(0, NX, go, 0)

    def fit_and_send(step, _):
        fit(step, 0)
        pl.when(step == 0)(lambda: forth(0, 0, 16))
        pl.when(step == 2)(lambda: forth(0, 16, 32))
        return 0

    lax.fori_loop(0, 4, fit_and_send, 0)
    tail = eight(8)
    sent[:, pl.ds(MAIN, 16), :] = jnp.concatenate(tail, axis=1).astype(jnp.bfloat16)
    forth(0, 48, 32)
    forth(1, None, None)
    own_forth = pltpu.make_async_copy(sent.at[my_p], landed.at[me], own_sem.at[2])
    own_forth.start()

    unit = 2.0 * math.pi / NX

    def signed(index):
        return jnp.where(index < NX // 2, index, index - NX).astype(jnp.float32) * unit

    along_a = signed(lax.broadcasted_iota(jnp.int32, (NX, NX), 1))
    along_c = signed(jnp.full((NX, NX), my_p, jnp.int32))
    base = along_a * along_a + along_c * along_c

    def build(kb, _):
        along_b = signed(jnp.full((NX, NX), kb, jnp.int32))
        squared = base + along_b * along_b
        weight = jnp.where(squared > 0, 1.0 / (squared + screening), 0.0)
        top, rest = split(basis_ref[...] * weight)
        table = terms_ref[...]
        full = dot(top, table[:, :NX]) + (dot(top, table[:, NX:]) + dot(rest, table[:, :NX]))
        top, rest = split(full)
        middle[kb] = jnp.concatenate([top, rest], axis=1)
        return 0

    lax.fori_loop(0, NX // 2 + 1, build, 0)
    total[...] = jnp.zeros_like(total)
    loads[1].wait()
    loads[2].wait()
    own_forth.wait()

    def respond(half, late, rank):
        def start(begin, size, target, sem):
            source = landed.at[rank, pl.ds(begin, size), :]
            sems = back_sem.at[sem]
            remote(source, target, sems.at[0], sems.at[1], rank).start()

        def at(begin, size):
            return back.at[my_p, pl.ds(begin, size), :]

        if late:
            start(112, 32, at(112, 32), 5)
            return

        @pl.when(on_first)
        def _():
            if half == 0:
                start(0, 64, at(0, 64), 0)
            else:
                start(64, 48, at(64, 48), 2)

        @pl.when(on_second)
        def _():
            if half == 0:
                start(0, 80, at(0, 80), 1)
            else:
                start(80, 32, at(80, 32), 3)
                start(64, 16, back_tail.at[chip // 2], 4)

    for half in range(2):
        active = on_first | (my_half == half)

        @pl.when(on_first)
        def _(half=half):
            bytes_of(landed, RANKS - 1, 80 if half == 0 else 64, forth_sem.at[half, 1])

        @pl.when(on_second & (my_half == half))
        def _(half=half):
            bytes_of(landed, RANKS - 1, 80, forth_sem.at[2 * half, 1])

        @pl.when(active)
        def _(half=half):
            solve(half, landed, field, middle, terms_ref)

            for late in range(1 + half):

                def answer(k, _, late=late):
                    respond(half, late, peer(k))
                    return 0

                lax.fori_loop(1, RANKS, answer, 0)

    def keep(test, pieces):
        @pl.when(test)
        def _():
            for i, (begin, size, target) in enumerate(pieces):
                source = landed.at[me, pl.ds(begin, size), :]
                copy = pltpu.make_async_copy(source, target, own_sem.at[3 + i])
                copy.start()
                copy.wait()

    mine_back = lambda begin, size: (begin, size, back.at[my_p, pl.ds(begin, size), :])
    keep(on_first, [mine_back(0, BLOCK)])
    keep(on_second & (my_half == 0), [mine_back(0, 80)])
    keep(on_second & (my_half == 1), [mine_back(80, 64), (64, 16, back_tail.at[chip // 2])])

    def left(test, count, size, sem):
        @pl.when(test)
        def _():
            bytes_of(sent, count, size, forth_sem.at[sem, 0])

    owns = on_first | (my_half == 0)
    left(owns, NX - 1, 80, 0)
    left(jnp.logical_not(owns), NX, 80, 0)
    left(on_first, CHIPS - 1, 64, 1)
    left(on_second, CHIPS, 64, 1)
    last = on_second & (my_half == 1)
    left(last, NX - CHIPS - 1, 80, 2)
    left(jnp.logical_not(last), NX - CHIPS, 80, 2)

    def arrived(test, count, size, sem, ref):
        @pl.when(test)
        def _():
            bytes_of(ref, count, size, back_sem.at[sem, 1])

    def potentials(blocks, half, first):
        turns = [block.reshape(TILE, 128).T for block in blocks]
        block = jnp.concatenate(turns, axis=0).astype(jnp.bfloat16)
        pot = (dot(block, high[...]) + dot(block, low[...])).astype(jnp.bfloat16)
        term = None
        for t in range(len(blocks)):
            here = pl.ds(pl.multiple_of((first + t) * TILE, TILE), TILE)
            some = pot[128 * t : 128 * t + 128]
            pot_ref[pl.ds(128 * half, 128), here] = some
            product = dot(some, pair[here, :])
            term = product if term is None else term + product
        total[pl.ds(128 * half, 128), :] += term

    for half in range(2):
        second = on_second & (my_half == half)
        def finish(s, _, half=half):
            lines = pl.ds(pl.multiple_of((80 if half else 0) + 16 * s, 16), 16)
            block = back[:, lines, :].astype(jnp.float32)
            potentials([block[:, :8], block[:, 8:]], half, 2 * s)
            return 0

        if half == 0:
            counts = ((0, 64, on_first, 64, back), (1, 32, second, 80, back))
        else:
            counts = ((2, 64, on_first, 48, back), (3, 32, second, 32, back), (4, 32, second, 16, back_tail))
        for sem, count, mine_too, size, ref in counts:
            arrived(mine_too, count - 1, size, sem, ref)
            arrived(jnp.logical_not(mine_too), count, size, sem, ref)
        if half == 0:
            lax.fori_loop(0, 4, finish, 0)
        else:
            lax.fori_loop(0, 2, finish, 0)
            block = back[:, pl.ds(MAIN, 16), :].astype(jnp.float32)
            other = back_tail[...].astype(jnp.float32)
            potentials([block[:, :8]], 0, 8)
            potentials([jnp.concatenate([block[:CHIPS, 8:], other[:, 8:]], axis=0)], 1, 8)
            late = on_first | second
            arrived(late, NX - 1, 32, 5, back)
            arrived(jnp.logical_not(late), NX, 32, 5, back)
            lax.fori_loop(2, 4, finish, 0)

    store = pltpu.make_async_copy(pot_ref, pot_hbm, load_sem.at[3])
    store.start()

    factor = math.sqrt(NMU) / float(NX**3)
    parts[...] = to_blocks(total[...].T * factor).astype(jnp.bfloat16)
    exchange(lambda d: parts.at[d], spread, sum_sem.at[1], own_sem.at[5])
    share = jnp.sum(spread[...].astype(jnp.float32), axis=0)
    part_ref[...] = jnp.concatenate([share[:8], share[8:]], axis=1)
    store.wait()

    def gone(test, size, sem):
        @pl.when(test)
        def _():
            bytes_of(landed, RANKS - 1, size, back_sem.at[sem, 0])

    gone(on_first, 64, 0)
    gone(on_first, 48, 2)
    gone(on_second & (my_half == 0), 80, 1)
    gone(on_second & (my_half == 1), 32, 3)
    gone(on_second & (my_half == 1), 16, 4)
    gone(on_first | (my_half == 1), 32, 5)


def solve(half, landed, field, middle, terms_ref):
    base = 80 if half else 0
    main, rest_of = pl.ds(base, MAIN), pl.ds(MAIN, 16)

    def block_of(rank):
        upper = landed[rank, main, :].astype(jnp.float32)
        lower = landed[rank, rest_of, :].astype(jnp.float32)[8 * half : 8 * half + 8]
        return jnp.concatenate([upper, lower], axis=0)

    def forward(i, _):
        for pack in range(2):
            start = 2 * i + pack
            wholes = [
                jnp.concatenate([block_of(8 * start + 4 * j + v) for v in range(4)], axis=0) for j in range(2)
            ]
            for plane in range(3):
                values = jnp.concatenate([w[96 * plane : 96 * plane + 96] for w in wholes], axis=1)
                result = dot(terms_ref[...], twice(values.astype(jnp.bfloat16)))
                for j in range(2):
                    field[3 * (2 * start + j) + plane] = result[:, 128 * j : 128 * j + 128]
        return 0

    lax.fori_loop(0, 8, forward, 0)

    def inner(i, _):
        place = pl.ds(pl.multiple_of(8 * i, 8), 8)
        values = jnp.swapaxes(field[:, place, :], 0, 1)
        results = []
        for j in range(8):
            kb = 8 * i + j
            table = middle[jnp.minimum(kb, NX - kb)]
            top, rest = split(values[j])
            results.append(dot(table, twice(top)) + dot(table[:, :NX], rest))
        field[:, place, :] = jnp.swapaxes(jnp.stack(results, axis=0), 0, 1)
        return 0

    lax.fori_loop(0, NX // 8, inner, 0)

    def backward(i, _):
        start = i
        planes = []
        for plane in range(3):
            values = jnp.concatenate([field[3 * (2 * start + j) + plane] for j in range(2)], axis=1)
            top, rest = split(values)
            planes.append(dot(terms_ref[...], twice(top)) + dot(terms_ref[:, :NX], rest))
        whole = jnp.concatenate(planes, axis=0)
        for j in range(2):
            for v in range(4):
                rank = 8 * start + 4 * j + v
                part = whole[OWN * v : OWN * v + OWN, 128 * j : 128 * j + 128]
                landed[rank, main, :] = part[:MAIN].astype(jnp.bfloat16)
                lower = landed[rank, rest_of, :].astype(jnp.float32)
                pieces = [part[MAIN:], lower[8:]] if half == 0 else [lower[:8], part[MAIN:]]
                landed[rank, rest_of, :] = jnp.concatenate(pieces, axis=0).astype(jnp.bfloat16)
        return 0

    lax.fori_loop(0, 16, backward, 0)


def everything(points, cinv, orbitals):
    table = basis(NX)
    high, low = line_tables()
    terms = np.concatenate(two_terms(table), axis=1)
    vmem = pl.BlockSpec(memory_space=pltpu.VMEM)
    hbm = pl.BlockSpec(memory_space=pl.ANY)
    bf, f32 = jnp.bfloat16, jnp.float32
    local_rows = orbitals.shape[0]
    dma = pltpu.SemaphoreType.DMA
    return pl.pallas_call(
        whole_kernel,
        out_shape=(
            jax.ShapeDtypeStruct((256, local_rows), bf),
            jax.ShapeDtypeStruct((8, 256), f32),
        ),
        in_specs=[vmem] * 4 + [hbm] * 3,
        out_specs=(hbm, vmem),
        scratch_shapes=[
            pltpu.VMEM((256, local_rows), bf),
            pltpu.VMEM((local_rows, 256), bf),
            pltpu.VMEM((TILE, TILE), bf),
            pltpu.VMEM((TILE, TILE), bf),
            pltpu.VMEM((local_rows, NMU), bf),
            pltpu.VMEM((NX, BLOCK, 128), bf),
            pltpu.VMEM((RANKS, BLOCK, 128), bf),
            pltpu.VMEM((NX, NX, 128), f32),
            pltpu.VMEM((NX, BLOCK, 128), bf),
            pltpu.VMEM((NX - CHIPS, 16, 128), bf),
            pltpu.VMEM((NMU, 256), bf),
            pltpu.VMEM((RANKS, 16, 128), bf),
            pltpu.VMEM((RANKS, 16, 128), bf),
            pltpu.VMEM((16, 128), bf),
            pltpu.VMEM((RANKS, 16, 128), bf),
            pltpu.VMEM((RANKS, 16, 128), bf),
            pltpu.VMEM((NX // 2 + 1, NX, 2 * NX), bf),
            pltpu.VMEM((256, NMU), f32),
            pltpu.VMEM((NMU, 256), f32),
            dma((2, 2)),
            dma((2,)),
            dma((3, 2)),
            dma((6, 2)),
            dma((6,)),
            dma((4,)),
        ],
        compiler_params=pltpu.CompilerParams(
            collective_id=0, has_side_effects=True, vmem_limit_bytes=58 * 2**20
        ),
    )(
        points, cinv, jnp.asarray(table.astype(np.float32)), jnp.asarray(terms),
        orbitals, jnp.asarray(high), jnp.asarray(low),
    )


def local(orbitals, points, cinv):
    return everything(points.reshape(NMU, 1), cinv, orbitals)


def solution(mesh):
    in_specs = (P(AXES, None), P(), P())
    out_specs = (P(None, AXES), P(AXES, None))
    return jax.shard_map(local, mesh=mesh, in_specs=in_specs, out_specs=out_specs, check_vma=False)
```

```python
import functools
import math

import jax
import jax.numpy as jnp
import ml_dtypes
import numpy as np
from jax import lax
from jax.experimental import pallas as pl
from jax.experimental.pallas import tpu as pltpu
from jax.sharding import PartitionSpec as P

NX = 96
NMU = 1024
RANKS = 128
CHIPS = 64
LINES = 8
TILE = LINES * NX
OWN = 72
MAIN = 64
BLOCK = 144
AXES = ("grid", "col")
MESH = pl.DeviceIdType.MESH

screening = 0.25


def rank_id():
    return lax.axis_index("grid") * 2 + lax.axis_index("col")


def device(rank):
    return {"grid": rank // 2, "col": lax.rem(rank, 2)}


def basis(size):
    index = np.arange(size)
    angle = (index[:, None] * index[None, :] % size) * (2.0 * math.pi / size)
    return (np.cos(angle) + np.sin(angle)) / math.sqrt(size)


def two_terms(table):
    high = table.astype(np.float32).astype(ml_dtypes.bfloat16)
    low = (table - high.astype(np.float64)).astype(np.float32).astype(ml_dtypes.bfloat16)
    return high, low


def line_tables():
    table = np.einsum("pc,lm->plmc", basis(NX), np.eye(LINES)).reshape(TILE, TILE)
    return two_terms(table)


def split(values):
    high = values.astype(jnp.bfloat16)
    return high, (values - high.astype(jnp.float32)).astype(jnp.bfloat16)


def dot(a, b):
    return jnp.dot(a, b, preferred_element_type=jnp.float32)


def twice(high):
    return jnp.concatenate([high, high], axis=0)


def parity_of(pair):
    return lax.rem(pair // 8 + pair // 2 + pair, 2)


def owner(p, half):
    pair = p - CHIPS
    first = p // 2 * 4 + lax.rem(p, 2)
    second = pair * 4 + 2 + lax.rem(half + parity_of(jnp.maximum(pair, 0)), 2)
    return jnp.where(p < CHIPS, first, second)


def whole_kernel(
    points_ref, cinv_ref, basis_ref, terms_ref, orb_hbm, high_hbm, low_hbm,
    pot_hbm, part_ref,
    pot_ref, orb, high, low, pair, sent, landed, field, back, back_tail,
    rows, picked, gathered, mine, spread, parts, middle, total, wide,
    sum_sem, all_sem, forth_sem, back_sem, own_sem, load_sem,
):
    me = rank_id()
    chip = me // 4 * 2 + lax.rem(me, 2)
    core = lax.rem(me // 2, 2)
    my_p = jnp.where(core == 0, chip, CHIPS + chip // 2)
    my_half = lax.rem(parity_of(chip // 2) + lax.rem(chip, 2), 2)
    on_first, on_second = core == 0, core == 1

    loads = [
        pltpu.make_async_copy(source, target, load_sem.at[i])
        for i, (source, target) in enumerate(((orb_hbm, orb), (high_hbm, high), (low_hbm, low)))
    ]
    for load in loads:
        load.start()

    def peer(k):
        return lax.rem(me + k * 53, RANKS)

    barrier = pltpu.get_barrier_semaphore()

    def greet(k, _):
        pl.semaphore_signal(barrier, inc=1, device_id=device(peer(k)), device_id_type=MESH)
        return 0

    lax.fori_loop(1, RANKS, greet, 0, unroll=4)

    def remote(source, target, send_sem, recv_sem, rank):
        return pltpu.make_async_remote_copy(
            src_ref=source,
            dst_ref=target,
            send_sem=send_sem,
            recv_sem=recv_sem,
            device_id=device(rank),
            device_id_type=MESH,
        )

    def bytes_of(ref, count, size, sem):
        block = ref.at[pl.ds(0, count), pl.ds(0, size), :]
        pltpu.make_async_copy(block, block, sem).wait()

    def exchange(source_of, target, sems, local_sem):
        local = pltpu.make_async_copy(source_of(me), target.at[me], local_sem)
        local.start()

        def go(k, _):
            rank = peer(k)
            remote(source_of(rank), target.at[me], sems.at[0], sems.at[1], rank).start()
            return 0

        lax.fori_loop(1, RANKS, go, 0, unroll=4)
        local.wait()
        bytes_of(target, RANKS - 1, 16, sems.at[0])
        bytes_of(target, RANKS - 1, 16, sems.at[1])

    def to_blocks(values):
        halves = [values[:, 128 * h : 128 * h + 128].reshape(RANKS, 8, 128) for h in range(2)]
        return jnp.concatenate(halves, axis=1)

    loads[0].wait()
    wide[...] = jnp.zeros_like(wide)

    def pick(step, _):
        here = pl.ds(pl.multiple_of(step * TILE, TILE), TILE)
        block = orb[here, :]
        for part in range(4):
            some = pl.ds(256 * part, 256)
            index = lax.broadcasted_iota(jnp.int32, (256, TILE), 1)
            match = index == (points_ref[some, :] - (me * orb.shape[0] + step * TILE))
            wide[some, :] += dot(jnp.where(match, 1.0, 0.0).astype(jnp.bfloat16), block)
        return 0

    lax.fori_loop(0, OWN // LINES, pick, 0)
    picked[...] = to_blocks(wide[...]).astype(jnp.bfloat16)
    pl.semaphore_wait(barrier, RANKS - 1)
    exchange(lambda d: picked.at[d], gathered, sum_sem.at[0], own_sem.at[0])
    mine[...] = jnp.sum(gathered[...].astype(jnp.float32), axis=0).astype(jnp.bfloat16)
    exchange(lambda d: mine, spread, all_sem, own_sem.at[1])
    whole = spread[...].astype(jnp.float32)
    whole = [whole[:, 8 * h : 8 * h + 8].reshape(NMU, 128) for h in range(2)]
    rows[...] = jnp.concatenate(whole, axis=1).astype(jnp.bfloat16)
    norms = jnp.sum(jnp.square(rows[...].astype(jnp.float32)), axis=1, keepdims=True)
    weights = norms * (jnp.sum(norms) * (1.0 / (NMU * 65536.0)))
    mean = jnp.sum(weights * cinv_ref[...].astype(jnp.float32), axis=0, keepdims=True)

    def eight(step):
        here = pl.ds(pl.multiple_of(step * TILE, TILE), TILE)
        product = lax.dot_general(
            orb[here, :], rows[...], (((1,), (1,)), ((), ())), preferred_element_type=jnp.float32
        ) * (1.0 / 16.0)
        squared = (product * product).astype(jnp.bfloat16)
        pair[here, :] = squared
        theta = dot(squared, cinv_ref[...]) - mean
        results = []
        for line in range(LINES):
            top, rest = split(theta[NX * line : NX * line + NX])
            results.append(dot(terms_ref[...], twice(top)) + dot(terms_ref[:, :NX], rest))
        return [
            jnp.swapaxes(jnp.stack([r[:, 128 * h : 128 * h + 128] for r in results], axis=0), 0, 1)
            for h in range(2)
        ]

    def fit(step, _):
        first, second = eight(2 * step), eight(2 * step + 1)
        for h, base in enumerate((0, MAIN + 16)):
            lines = pl.ds(pl.multiple_of(base + 16 * step, 16), 16)
            sent[:, lines, :] = jnp.concatenate([first[h], second[h]], axis=1).astype(jnp.bfloat16)
        return 0

    first_p = me * NX // RANKS

    def forth(half, begin, size):
        def go(k, _):
            p = lax.rem(first_p + k * 53, NX)
            rank = owner(p, half)

            def start(begin, size, sem):
                lines = pl.ds(begin, size)
                sems = forth_sem.at[sem]
                remote(sent.at[p, lines, :], landed.at[me, lines, :], sems.at[0], sems.at[1], rank).start()

            if half == 0:
                pl.when(rank != me)(lambda: start(begin, size, 0))
            else:
                pl.when((rank != me) & (p < CHIPS))(lambda: start(80, 64, 1))
                pl.when((rank != me) & (p >= CHIPS))(lambda: start(64, 80, 2))
            return 0

        lax.fori_loop(0, NX, go, 0, unroll=4)

    def fit_and_send(step, _):
        fit(step, 0)
        pl.when(step == 0)(lambda: forth(0, 0, 16))
        pl.when(step == 2)(lambda: forth(0, 16, 32))
        return 0

    lax.fori_loop(0, 4, fit_and_send, 0)
    tail = eight(8)
    sent[:, pl.ds(MAIN, 16), :] = jnp.concatenate(tail, axis=1).astype(jnp.bfloat16)
    forth(0, 48, 32)
    forth(1, None, None)
    own_forth = pltpu.make_async_copy(sent.at[my_p], landed.at[me], own_sem.at[2])
    own_forth.start()

    unit = 2.0 * math.pi / NX

    def signed(index):
        return jnp.where(index < NX // 2, index, index - NX).astype(jnp.float32) * unit

    along_a = signed(lax.broadcasted_iota(jnp.int32, (NX, NX), 1))
    along_c = signed(jnp.full((NX, NX), my_p, jnp.int32))
    base = along_a * along_a + along_c * along_c

    def build(kb, _):
        along_b = signed(jnp.full((NX, NX), kb, jnp.int32))
        squared = base + along_b * along_b
        weight = jnp.where(squared > 0, 1.0 / (squared + screening), 0.0)
        top, rest = split(basis_ref[...] * weight)
        table = terms_ref[...]
        full = dot(top, table[:, :NX]) + (dot(top, table[:, NX:]) + dot(rest, table[:, :NX]))
        top, rest = split(full)
        middle[kb] = jnp.concatenate([top, rest], axis=1)
        return 0

    lax.fori_loop(0, NX // 2 + 1, build, 0)
    total[...] = jnp.zeros_like(total)
    loads[1].wait()
    loads[2].wait()
    own_forth.wait()

    def respond(half, late, rank):
        def start(begin, size, target, sem):
            source = landed.at[rank, pl.ds(begin, size), :]
            sems = back_sem.at[sem]
            remote(source, target, sems.at[0], sems.at[1], rank).start()

        def at(begin, size):
            return back.at[my_p, pl.ds(begin, size), :]

        if late:
            start(112, 32, at(112, 32), 5)
            return

        @pl.when(on_first)
        def _():
            if half == 0:
                start(0, 64, at(0, 64), 0)
            else:
                start(64, 48, at(64, 48), 2)

        @pl.when(on_second)
        def _():
            if half == 0:
                start(0, 80, at(0, 80), 1)
            else:
                start(80, 32, at(80, 32), 3)
                start(64, 16, back_tail.at[chip // 2], 4)

    for half in range(2):
        active = on_first | (my_half == half)

        @pl.when(on_first)
        def _(half=half):
            bytes_of(landed, RANKS - 1, 80 if half == 0 else 64, forth_sem.at[half, 1])

        @pl.when(on_second & (my_half == half))
        def _(half=half):
            bytes_of(landed, RANKS - 1, 80, forth_sem.at[2 * half, 1])

        @pl.when(active)
        def _(half=half):
            solve(half, landed, field, middle, terms_ref)

            for late in range(1 + half):

                def answer(k, _, late=late):
                    respond(half, late, peer(k))
                    return 0

                lax.fori_loop(1, RANKS, answer, 0, unroll=4)

    def keep(test, pieces):
        @pl.when(test)
        def _():
            for i, (begin, size, target) in enumerate(pieces):
                source = landed.at[me, pl.ds(begin, size), :]
                copy = pltpu.make_async_copy(source, target, own_sem.at[3 + i])
                copy.start()
                copy.wait()

    mine_back = lambda begin, size: (begin, size, back.at[my_p, pl.ds(begin, size), :])
    keep(on_first, [mine_back(0, BLOCK)])
    keep(on_second & (my_half == 0), [mine_back(0, 80)])
    keep(on_second & (my_half == 1), [mine_back(80, 64), (64, 16, back_tail.at[chip // 2])])

    def left(test, count, size, sem):
        @pl.when(test)
        def _():
            bytes_of(sent, count, size, forth_sem.at[sem, 0])

    owns = on_first | (my_half == 0)
    left(owns, NX - 1, 80, 0)
    left(jnp.logical_not(owns), NX, 80, 0)
    left(on_first, CHIPS - 1, 64, 1)
    left(on_second, CHIPS, 64, 1)
    last = on_second & (my_half == 1)
    left(last, NX - CHIPS - 1, 80, 2)
    left(jnp.logical_not(last), NX - CHIPS, 80, 2)

    def arrived(test, count, size, sem, ref):
        @pl.when(test)
        def _():
            bytes_of(ref, count, size, back_sem.at[sem, 1])

    def potentials(blocks, half, first):
        turns = [block.reshape(TILE, 128).T for block in blocks]
        block = jnp.concatenate(turns, axis=0).astype(jnp.bfloat16)
        pot = (dot(block, high[...]) + dot(block, low[...])).astype(jnp.bfloat16)
        term = None
        for t in range(len(blocks)):
            here = pl.ds(pl.multiple_of((first + t) * TILE, TILE), TILE)
            some = pot[128 * t : 128 * t + 128]
            pot_ref[pl.ds(128 * half, 128), here] = some
            product = dot(some, pair[here, :])
            term = product if term is None else term + product
        total[pl.ds(128 * half, 128), :] += term

    for half in range(2):
        second = on_second & (my_half == half)
        def finish(s, _, half=half):
            lines = pl.ds(pl.multiple_of((80 if half else 0) + 16 * s, 16), 16)
            block = back[:, lines, :].astype(jnp.float32)
            potentials([block[:, :8], block[:, 8:]], half, 2 * s)
            return 0

        if half == 0:
            counts = ((0, 64, on_first, 64, back), (1, 32, second, 80, back))
        else:
            counts = ((2, 64, on_first, 48, back), (3, 32, second, 32, back), (4, 32, second, 16, back_tail))
        for sem, count, mine_too, size, ref in counts:
            arrived(mine_too, count - 1, size, sem, ref)
            arrived(jnp.logical_not(mine_too), count, size, sem, ref)
        if half == 0:
            lax.fori_loop(0, 4, finish, 0)
        else:
            lax.fori_loop(0, 2, finish, 0)
            block = back[:, pl.ds(MAIN, 16), :].astype(jnp.float32)
            other = back_tail[...].astype(jnp.float32)
            potentials([block[:, :8]], 0, 8)
            potentials([jnp.concatenate([block[:CHIPS, 8:], other[:, 8:]], axis=0)], 1, 8)
            late = on_first | second
            arrived(late, NX - 1, 32, 5, back)
            arrived(jnp.logical_not(late), NX, 32, 5, back)
            lax.fori_loop(2, 4, finish, 0)

    store = pltpu.make_async_copy(pot_ref, pot_hbm, load_sem.at[3])
    store.start()

    factor = math.sqrt(NMU) / float(NX**3)
    parts[...] = to_blocks(total[...].T * factor).astype(jnp.bfloat16)
    exchange(lambda d: parts.at[d], spread, sum_sem.at[1], own_sem.at[5])
    share = jnp.sum(spread[...].astype(jnp.float32), axis=0)
    part_ref[...] = jnp.concatenate([share[:8], share[8:]], axis=1)
    store.wait()

    def gone(test, size, sem):
        @pl.when(test)
        def _():
            bytes_of(landed, RANKS - 1, size, back_sem.at[sem, 0])

    gone(on_first, 64, 0)
    gone(on_first, 48, 2)
    gone(on_second & (my_half == 0), 80, 1)
    gone(on_second & (my_half == 1), 32, 3)
    gone(on_second & (my_half == 1), 16, 4)
    gone(on_first | (my_half == 1), 32, 5)


def solve(half, landed, field, middle, terms_ref):
    base = 80 if half else 0
    main, rest_of = pl.ds(base, MAIN), pl.ds(MAIN, 16)

    def block_of(rank):
        upper = landed[rank, main, :].astype(jnp.float32)
        lower = landed[rank, rest_of, :].astype(jnp.float32)[8 * half : 8 * half + 8]
        return jnp.concatenate([upper, lower], axis=0)

    def forward(i, _):
        for pack in range(2):
            start = 2 * i + pack
            wholes = [
                jnp.concatenate([block_of(8 * start + 4 * j + v) for v in range(4)], axis=0) for j in range(2)
            ]
            for plane in range(3):
                values = jnp.concatenate([w[96 * plane : 96 * plane + 96] for w in wholes], axis=1)
                result = dot(terms_ref[...], twice(values.astype(jnp.bfloat16)))
                for j in range(2):
                    field[3 * (2 * start + j) + plane] = result[:, 128 * j : 128 * j + 128]
        return 0

    lax.fori_loop(0, 8, forward, 0)

    def inner(i, _):
        place = pl.ds(pl.multiple_of(8 * i, 8), 8)
        values = jnp.swapaxes(field[:, place, :], 0, 1)
        results = []
        for j in range(8):
            kb = 8 * i + j
            table = middle[jnp.minimum(kb, NX - kb)]
            top, rest = split(values[j])
            results.append(dot(table, twice(top)) + dot(table[:, :NX], rest))
        field[:, place, :] = jnp.swapaxes(jnp.stack(results, axis=0), 0, 1)
        return 0

    lax.fori_loop(0, NX // 8, inner, 0)

    def backward(i, _):
        start = i
        planes = []
        for plane in range(3):
            values = jnp.concatenate([field[3 * (2 * start + j) + plane] for j in range(2)], axis=1)
            top, rest = split(values)
            planes.append(dot(terms_ref[...], twice(top)) + dot(terms_ref[:, :NX], rest))
        whole = jnp.concatenate(planes, axis=0)
        for j in range(2):
            for v in range(4):
                rank = 8 * start + 4 * j + v
                part = whole[OWN * v : OWN * v + OWN, 128 * j : 128 * j + 128]
                landed[rank, main, :] = part[:MAIN].astype(jnp.bfloat16)
                lower = landed[rank, rest_of, :].astype(jnp.float32)
                pieces = [part[MAIN:], lower[8:]] if half == 0 else [lower[:8], part[MAIN:]]
                landed[rank, rest_of, :] = jnp.concatenate(pieces, axis=0).astype(jnp.bfloat16)
        return 0

    lax.fori_loop(0, 16, backward, 0)


def everything(points, cinv, orbitals):
    table = basis(NX)
    high, low = line_tables()
    terms = np.concatenate(two_terms(table), axis=1)
    vmem = pl.BlockSpec(memory_space=pltpu.VMEM)
    hbm = pl.BlockSpec(memory_space=pl.ANY)
    bf, f32 = jnp.bfloat16, jnp.float32
    local_rows = orbitals.shape[0]
    dma = pltpu.SemaphoreType.DMA
    return pl.pallas_call(
        whole_kernel,
        out_shape=(
            jax.ShapeDtypeStruct((256, local_rows), bf),
            jax.ShapeDtypeStruct((8, 256), f32),
        ),
        in_specs=[vmem] * 4 + [hbm] * 3,
        out_specs=(hbm, vmem),
        scratch_shapes=[
            pltpu.VMEM((256, local_rows), bf),
            pltpu.VMEM((local_rows, 256), bf),
            pltpu.VMEM((TILE, TILE), bf),
            pltpu.VMEM((TILE, TILE), bf),
            pltpu.VMEM((local_rows, NMU), bf),
            pltpu.VMEM((NX, BLOCK, 128), bf),
            pltpu.VMEM((RANKS, BLOCK, 128), bf),
            pltpu.VMEM((NX, NX, 128), f32),
            pltpu.VMEM((NX, BLOCK, 128), bf),
            pltpu.VMEM((NX - CHIPS, 16, 128), bf),
            pltpu.VMEM((NMU, 256), bf),
            pltpu.VMEM((RANKS, 16, 128), bf),
            pltpu.VMEM((RANKS, 16, 128), bf),
            pltpu.VMEM((16, 128), bf),
            pltpu.VMEM((RANKS, 16, 128), bf),
            pltpu.VMEM((RANKS, 16, 128), bf),
            pltpu.VMEM((NX // 2 + 1, NX, 2 * NX), bf),
            pltpu.VMEM((256, NMU), f32),
            pltpu.VMEM((NMU, 256), f32),
            dma((2, 2)),
            dma((2,)),
            dma((3, 2)),
            dma((6, 2)),
            dma((6,)),
            dma((4,)),
        ],
        compiler_params=pltpu.CompilerParams(
            collective_id=0, has_side_effects=True, vmem_limit_bytes=58 * 2**20
        ),
    )(
        points, cinv, jnp.asarray(table.astype(np.float32)), jnp.asarray(terms),
        orbitals, jnp.asarray(high), jnp.asarray(low),
    )


def local(orbitals, points, cinv):
    return everything(points.reshape(NMU, 1), cinv, orbitals)


def solution(mesh):
    in_specs = (P(AXES, None), P(), P())
    out_specs = (P(None, AXES), P(AXES, None))
    return jax.shard_map(local, mesh=mesh, in_specs=in_specs, out_specs=out_specs, check_vma=False)
```
